32 devices in a mesh: resp: 8 (over z, core), seq: 4 (over y, x).
Axes of the slice: x: 2, y: 2, z: 4, core: 2. Of those that a mesh axis runs over, the one named last changes fastest.
Arguments:
- prompt_cache: bfloat16 [512, 576], P('seq'), may hold values from -8 to 8
- channel_scale: float32 [576], replicated, may hold values from 0.5 to 2
- span_cache: bfloat16 [512, 576], P('resp'), may hold values from -6 to 6
- q_latent: bfloat16 [512, 128, 512], P('resp', 'seq'), may hold values from -6 to 6
- q_rope: bfloat16 [512, 8192], P('resp', 'seq'), may hold values from -512 to 512
- d_out: bfloat16 [512, 128, 512], P('resp', 'seq'), may hold values from -6 to 6
- resp_length: int32 [16], replicated, may hold values from 1 to 16384
- span_response: int32 [8], replicated, may hold values from 0 to 15
- span_index: int32 [8], replicated, may hold values from 0 to 255
Outputs:
- grad_q_latent: bfloat16 [512, 128, 512], P('resp', 'seq')
- grad_q_rope: bfloat16 [512, 8192], P('resp', 'seq')
- grad_prompt: float32 [512, 576], P('seq', 'resp')
- grad_span: float32 [512, 576], P(('resp', 'seq'))
The draws below stay inside these ranges and needn't reach their ends.
All inputs are finite; a program needn't handle non-finite values.
Results may differ from the reference program's by a relative error of at most 0.029.
Values may be sent and summed in bfloat16 or wider, within the bound.
No kernel may reach another device: no remote copies, remote signals or barrier semaphores. Data moves between devices by JAX's collectives and lax.ppermute only.
A program may use at most 64 MiB of HBM per device.

```python
import math
import jax
import jax.numpy as jnp
from jax import lax

HEADS = 128
LATENT = 512
ROPE = 64
RESPONSES = 16
MAXCHUNK = 256
TOK_DEV = 64
PROMPT = 512
TOKENS = 512
RESP_LEN = 16384
N_RESP = 8
N_SEQ = 4


def prompt_table(key):
    base = jax.random.normal(jax.random.fold_in(key, 11), (PROMPT, LATENT + ROPE), jnp.float32)
    base = jnp.clip(base, -6.0, 6.0)
    return base


def draw_prompt_cache(key, part):
    return prompt_table(key).astype(jnp.bfloat16)


def draw_q_rope(key, part):
    values = jax.random.normal(jax.random.fold_in(key, 21), (TOKENS, HEADS * ROPE), jnp.float32)
    values = jnp.clip(values, -6.0, 6.0)
    return values.astype(jnp.bfloat16)


def place_ends(result, rng, low, top_value):
    index_at = [jax.random.randint(jax.random.fold_in(rng, axis), (), 0, length) for axis, length in enumerate(result.shape)]
    widest = result.shape.index(max(result.shape))
    beside = index_at[:widest] + [(index_at[widest] + 1) % result.shape[widest]] + index_at[widest + 1:]
    return result.at[tuple(index_at)].set(low).at[tuple(beside)].set(top_value)


def block_levels(own_key, shape, shards, low, largest):
    gain, own = 1.0, jax.random.fold_in(own_key, 6)
    for position, parts in shards:
        draws = jnp.exp(jax.random.uniform(jax.random.fold_in(own, position), (parts,), jnp.float32, low / len(shards), largest / len(shards)))
        gain = gain * jnp.repeat(draws, shape[position] // parts).reshape([-1 if axis == position else 1 for axis in range(len(shape))])
    return gain


def gaussian(own_key, dims, spread, reach, pieces=(), kind=jnp.bfloat16):
    entries = spread * jax.random.normal(own_key, dims, jnp.float32)
    if pieces:
        entries = entries * block_levels(own_key, dims, pieces, -0.22, 0.18)
    return jnp.clip(entries, -reach, reach).astype(kind)


def setup_inputs(seed: int = 0) -> dict:
    keys = jax.random.split(jax.random.key(seed), 10)
    prompt_cache = draw_prompt_cache(jax.random.fold_in(keys[9], 71), 0)
    channel_scale = jnp.clip(jnp.exp(jax.random.uniform(keys[1], (LATENT + ROPE,), jnp.float32, math.log(0.5), math.log(2.0))), 0.5, 2.0)
    span_cache = gaussian(keys[2], (TOKENS, LATENT + ROPE), 1.0, 6.0, ((0, 8),))
    q_latent = gaussian(keys[3], (TOKENS, HEADS, LATENT), 1.0, 6.0, ((0, 8), (1, 4)))
    q_rope = draw_q_rope(jax.random.fold_in(keys[9], 71), 0)
    d_out = gaussian(keys[5], (TOKENS, HEADS, LATENT), 1.0, 6.0, ((0, 8), (1, 4)))
    resp_length = place_ends(jax.random.randint(keys[6], (RESPONSES,), 1, RESP_LEN + 1), jax.random.fold_in(keys[6], 1), 1, RESP_LEN).astype(jnp.int32)
    span_response = place_ends(jax.random.randint(keys[7], (N_RESP,), 0, RESPONSES), jax.random.fold_in(keys[7], 1), 0, RESPONSES - 1).astype(jnp.int32)
    span_index = place_ends(jax.random.randint(keys[8], (N_RESP,), 0, MAXCHUNK), jax.random.fold_in(keys[8], 1), 0, MAXCHUNK - 1).astype(jnp.int32)
    return {"prompt_cache": prompt_cache, "channel_scale": channel_scale, "span_cache": span_cache, "q_latent": q_latent, "q_rope": q_rope, "d_out": d_out, "resp_length": resp_length, "span_response": span_response, "span_index": span_index}


SIGMA = 1.0 / math.sqrt(192.0)

def grouped(values):
    return values.reshape(values.shape[0], N_SEQ, HEADS // N_SEQ, values.shape[-1])

def block_backward(prompt_keys, block_keys, query_latent, query_rope, cotangent, live_count):
    all_keys = jnp.concatenate([prompt_keys, block_keys], axis=0).astype(jnp.float32)
    latent_keys = all_keys[:, :LATENT]
    rotary_keys = all_keys[:, LATENT:]
    query_pos = lax.broadcasted_iota(jnp.int32, (TOK_DEV, TOK_DEV), 0)
    key_pos = lax.broadcasted_iota(jnp.int32, (TOK_DEV, TOK_DEV), 1)
    block_seen = (key_pos <= query_pos) & (key_pos < live_count)
    visible = jnp.concatenate([jnp.ones((TOK_DEV, PROMPT), bool), block_seen], axis=1)
    latent_q = query_latent.astype(jnp.float32)
    rotary_q = query_rope.astype(jnp.float32)
    logits = SIGMA * (jnp.einsum('thc,kc->thk', latent_q, latent_keys) + jnp.einsum('thc,kc->thk', rotary_q, rotary_keys))
    masked = jnp.where(visible[:, None, :], logits, -jnp.inf)
    highest = lax.optimization_barrier(jnp.max(masked, axis=2, keepdims=True))
    expo = jnp.where(visible[:, None, :], jnp.exp(logits - highest), 0.0)
    probs = expo / lax.optimization_barrier(jnp.sum(expo, axis=2, keepdims=True))
    probs_half = probs.astype(jnp.bfloat16).astype(jnp.float32)
    valid = lax.iota(jnp.int32, TOK_DEV) < live_count
    upstream = jnp.where(valid[:, None, None], cotangent, jnp.zeros_like(cotangent)).astype(jnp.float32)
    attended = jnp.einsum('thk,kc->thc', probs_half, latent_keys)
    delta = lax.optimization_barrier(jnp.sum(upstream * attended, axis=2, keepdims=True))
    dprob = jnp.einsum('thc,kc->thk', upstream, latent_keys)
    dscore = (probs * (dprob - delta)).astype(jnp.bfloat16).astype(jnp.float32)
    grad_latent = (SIGMA * jnp.einsum('thk,kc->thc', dscore, latent_keys)).astype(jnp.bfloat16)
    grad_rotary = (SIGMA * jnp.einsum('thk,kc->thc', dscore, rotary_keys)).astype(jnp.bfloat16)
    score_block = dscore[:, :, PROMPT:]
    prob_block = probs_half[:, :, PROMPT:]
    block_latent = SIGMA * jnp.einsum('thk,thc->kc', score_block, latent_q) + jnp.einsum('thk,thc->kc', prob_block, upstream)
    block_rotary = SIGMA * jnp.einsum('thk,thc->kc', score_block, rotary_q)
    block_grad = jnp.concatenate([block_latent, block_rotary], axis=1)
    score_prompt = grouped(dscore[:, :, :PROMPT])
    prob_prompt = grouped(probs_half[:, :, :PROMPT])
    prompt_latent = SIGMA * jnp.einsum('tghk,tghc->gkc', score_prompt, grouped(latent_q)) + jnp.einsum('tghk,tghc->gkc', prob_prompt, grouped(upstream))
    prompt_rotary = SIGMA * jnp.einsum('tghk,tghc->gkc', score_prompt, grouped(rotary_q))
    prompt_terms = jnp.concatenate([prompt_latent, prompt_rotary], axis=2).astype(jnp.bfloat16).astype(jnp.float32)
    return (grad_latent, grad_rotary, lax.optimization_barrier(jnp.sum(prompt_terms, axis=0)), block_grad)

def reference(prompt_cache, channel_scale, span_cache, q_latent, q_rope, d_out, resp_length, span_response, span_index):
    prompt_keys = (prompt_cache.astype(jnp.float32) * channel_scale).astype(jnp.bfloat16)
    live = jnp.clip(resp_length[span_response] - span_index * TOK_DEV, 0, TOK_DEV).astype(jnp.int32)
    width = LATENT + ROPE
    block_keys = span_cache.reshape(N_RESP, TOK_DEV, width)
    latent_all = q_latent.reshape(N_RESP, TOK_DEV, HEADS, LATENT)
    rotary_all = q_rope.reshape(N_RESP, TOK_DEV, HEADS, ROPE)
    upstream_all = d_out.reshape(N_RESP, TOK_DEV, HEADS, LATENT)

    def step(accum, items):
        keys_here, latent_here, rotary_here, upstream_here, live_here = items
        grad_latent, grad_rotary, prompt_part, block_part = block_backward(prompt_keys, keys_here, latent_here, rotary_here, upstream_here, live_here)
        return (accum + prompt_part, (grad_latent, grad_rotary, block_part))
    start = jnp.zeros((PROMPT, width), jnp.float32)
    summed, (grad_latent, grad_rotary, block_grads) = lax.scan(step, start, (block_keys, latent_all, rotary_all, upstream_all, live))
    grad_prompt = summed * channel_scale
    return (grad_latent.reshape(TOKENS, HEADS, LATENT), grad_rotary.reshape(TOKENS, HEADS * ROPE), grad_prompt, block_grads.reshape(TOKENS, width))
```

```python
import functools
import math

import jax
import jax.numpy as jnp
from jax import lax
from jax.experimental import pallas as pl
from jax.experimental.pallas import tpu as pltpu
from jax.sharding import PartitionSpec as P

SIGMA = 1.0 / math.sqrt(192.0)
LOG2E = math.log2(math.e)
F32 = jnp.float32
BF16 = jnp.bfloat16
NT = (((1,), (1,)), ((), ()))
NN = (((1,), (0,)), ((), ()))
TN = (((0,), (0,)), ((), ()))


def dot(a, b, dims):
    return lax.dot_general(a, b, dims, preferred_element_type=F32)


def low_half(shape, half):
    return lax.broadcasted_iota(jnp.int32, shape, len(shape) - 1) < half


def keys_kernel(
    n_resp,
    n_seq,
    heads,
    resp_length,
    span_response,
    span_index,
    scale_ref,
    span_ref,
    q_ref,
    qrope_ref,
    up_ref,
    *refs,
):
    shard_refs = refs[:n_seq]
    mine_ref, theirs_ref, span_out, ds_ref, keys_ref = refs[n_seq : n_seq + 5]
    rope_scr, p_scr, qr_ref = refs[n_seq + 5 :]
    tok, full = span_ref.shape
    rows, latent = q_ref.shape
    rope = full - latent
    shard = shard_refs[0].shape[0]
    prompt = shard * n_seq
    keys = prompt + tok
    my_resp = lax.axis_index("resp")
    my_seq = lax.axis_index("seq")
    live = jnp.clip(
        resp_length[span_response[my_resp]] - span_index[my_resp] * tok, 0, tok
    )

    scale = scale_ref[...]
    for d in range(n_seq):
        k = (shard_refs[d][...].astype(F32) * scale).astype(BF16)
        keys_ref[pl.ds(d * shard, shard), :full] = k
        keys_ref[pl.ds(d * shard, shard), full:] = k[:, latent:]
    keys_ref[pl.ds(prompt, tok), :full] = span_ref[...]
    keys_ref[pl.ds(prompt, tok), full:] = span_ref[:, latent:]

    low = low_half((tok, 2 * rope), rope)
    for j in range(heads // 2):
        x = qrope_ref[:, pl.ds(2 * rope * j, 2 * rope)].astype(F32)
        rope_scr[pl.ds(2 * j, tok, stride=heads), :] = jnp.where(low, x, 0.0)
        rope_scr[pl.ds(2 * j + 1, tok, stride=heads), :] = jnp.where(low, 0.0, x)
    qr_ref[...] = rope_scr[...].astype(BF16)

    step = 256
    for i in range(rows // step):
        at = pl.ds(i * step, step)
        logits = dot(keys_ref[:, :latent], q_ref[at, :], NT) + dot(
            keys_ref[:, latent:], qr_ref[at, :], NT
        )
        dprob = dot(keys_ref[:, :latent], up_ref[at, :], NT)
        key_pos = lax.broadcasted_iota(jnp.int32, (tok, step), 0)
        query_pos = (lax.broadcasted_iota(jnp.int32, (tok, step), 1) + i * step) // heads
        seen = (key_pos <= query_pos) & (key_pos < live)
        own = jnp.where(seen, logits[prompt:], -jnp.inf)
        logits = jnp.concatenate([logits[:prompt], own], axis=0)
        top = jnp.max(logits, axis=0, keepdims=True)
        expo = jnp.exp2((logits - top) * (SIGMA * LOG2E))
        total = jnp.sum(expo, axis=0, keepdims=True)
        weighed = jnp.sum(expo * dprob, axis=0, keepdims=True)
        row_pos = (lax.broadcasted_iota(jnp.int32, (1, step), 1) + i * step) // heads
        inverse = 1.0 / total
        delta = weighed * inverse
        inverse = jnp.where(row_pos < live, inverse, 0.0)
        probs = expo * inverse
        p_scr[:, at] = probs.astype(BF16)
        ds_ref[:, at] = (probs * ((dprob - delta) * SIGMA)).astype(BF16)

    grad_latent = dot(ds_ref[...], q_ref[...], NN) + dot(p_scr[...], up_ref[...], NN)
    grad_rope = dot(ds_ref[...], qr_ref[...], NN)

    piece = tok // n_seq
    own_rope = grad_rope[prompt:]
    own_rope = own_rope + pltpu.roll(own_rope, rope, 1)
    for s in range(n_seq):
        parts = [
            grad_latent[prompt + s * piece : prompt + (s + 1) * piece, c : c + 2 * rope]
            for c in range(0, latent, 2 * rope)
        ]
        parts.append(own_rope[s * piece : (s + 1) * piece])
        span_out[s ^ my_seq] = jnp.concatenate(parts, axis=0).astype(BF16)

    cols = full // n_resp
    odd = (my_resp % 2) == 1
    my_pair = my_resp // 2
    for d in range(n_seq):
        at = slice(d * shard, (d + 1) * shard)
        lat = grad_latent[at].T
        rot = grad_rope[at].T
        whole = jnp.concatenate([lat, rot[:rope] + rot[rope:]], axis=0)
        for z in range(n_resp // 2):
            even_part = whole[2 * z * cols : (2 * z + 1) * cols]
            odd_part = whole[(2 * z + 1) * cols : (2 * z + 2) * cols]
            mine_ref[d, z ^ my_pair] = jnp.where(odd, odd_part, even_part).astype(BF16)
            theirs_ref[d, z ^ my_pair] = jnp.where(odd, even_part, odd_part).astype(BF16)


def query_kernel(heads, ds_ref, keys_ref, out_ref, rope_out, rope_scr):
    rows, latent = out_ref.shape
    width = keys_ref.shape[1]
    rope = (width - latent) // 2
    step = 16 * heads
    for i in range(rows // step):
        at = pl.ds(i * step, step)
        out_ref[at, :] = dot(ds_ref[:, at], keys_ref[:, :latent], TN).astype(BF16)
        rope_scr[...] = dot(ds_ref[:, at], keys_ref[:, latent:], TN)
        low = low_half((16, 2 * rope), rope)
        for j in range(heads // 2):
            even = rope_scr[pl.ds(2 * j, 16, stride=heads), :]
            odd = rope_scr[pl.ds(2 * j + 1, 16, stride=heads), :]
            rope_out[pl.ds(i * 16, 16), pl.ds(2 * rope * j, 2 * rope)] = jnp.where(
                low, even, odd
            ).astype(BF16)


def on_device(
    n_resp,
    n_seq,
    prompt_cache,
    channel_scale,
    span_cache,
    q_latent,
    q_rope,
    d_out,
    resp_length,
    span_response,
    span_index,
):
    tok, heads, latent = q_latent.shape
    shard, full = prompt_cache.shape
    rope = full - latent
    rows = tok * heads
    prompt = shard * n_seq
    keys = prompt + tok
    width = latent + 2 * rope
    cols = full // n_resp
    pairs = n_resp // 2
    piece = tok // n_seq
    span_rows = piece * (latent // (2 * rope) + 1)

    def over_seq(x, d):
        return lax.ppermute(x, "seq", [(i, i ^ d) for i in range(n_seq)])

    def over_resp(x, d):
        return lax.ppermute(x, "resp", [(i, i ^ d) for i in range(n_resp)])

    order = sorted(range(1, n_seq), key=lambda d: -bin(d).count("1"))
    got = {d: over_seq(prompt_cache, d) for d in order}
    shards = [prompt_cache] + [got[d] for d in range(1, n_seq)]

    vmem = pl.BlockSpec(memory_space=pltpu.VMEM)
    smem = pl.BlockSpec(memory_space=pltpu.SMEM)
    q_rows = q_latent.reshape(rows, latent)
    up_rows = d_out.reshape(rows, latent)
    mine, theirs, span, dscore, keys_all = pl.pallas_call(
        functools.partial(keys_kernel, n_resp, n_seq, heads),
        out_shape=(
            jax.ShapeDtypeStruct((n_seq, pairs, cols, shard), BF16),
            jax.ShapeDtypeStruct((n_seq, pairs, cols, shard), BF16),
            jax.ShapeDtypeStruct((n_seq, span_rows, 2 * rope), BF16),
            jax.ShapeDtypeStruct((keys, rows), BF16),
            jax.ShapeDtypeStruct((keys, width), BF16),
        ),
        in_specs=[smem] * 3 + [vmem] * (5 + n_seq),
        out_specs=(vmem,) * 5,
        scratch_shapes=[
            pltpu.VMEM((rows, 2 * rope), F32),
            pltpu.VMEM((keys, rows), BF16),
            pltpu.VMEM((rows, 2 * rope), BF16),
        ],
        compiler_params=pltpu.CompilerParams(vmem_limit_bytes=48 * 1024 * 1024),
        cost_estimate=pl.CostEstimate(
            flops=2 * keys * rows * 4 * latent, bytes_accessed=6 * rows * latent, transcendentals=0
        ),
        name="keys",
    )(
        resp_length,
        span_response,
        span_index,
        channel_scale.reshape(1, full),
        span_cache,
        q_rows,
        q_rope,
        up_rows,
        *shards,
    )

    grad_latent, grad_rope = pl.pallas_call(
        functools.partial(query_kernel, heads),
        out_shape=(
            jax.ShapeDtypeStruct((rows, latent), BF16),
            jax.ShapeDtypeStruct((tok, heads * rope), BF16),
        ),
        in_specs=[vmem] * 2,
        out_specs=(vmem,) * 2,
        scratch_shapes=[pltpu.VMEM((16 * heads, 2 * rope), F32)],
        compiler_params=pltpu.CompilerParams(vmem_limit_bytes=32 * 1024 * 1024),
        cost_estimate=pl.CostEstimate(
            flops=2 * keys * rows * width, bytes_accessed=6 * rows * latent, transcendentals=0
        ),
        name="queries",
    )(dscore, keys_all)

    summed = mine.astype(F32) + over_resp(theirs, 1).astype(F32)
    held = summed.astype(BF16).reshape(n_seq, pairs * cols, shard)
    moved = {
        d: over_seq(
            jnp.concatenate(
                [held[d].reshape(-1, 2 * rope), span[d]], axis=0
            ),
            d,
        )
        for d in order
    }
    split = pairs * cols * shard // (2 * rope)
    block = summed[0].reshape(pairs, cols, shard)
    own = span[0].astype(F32)
    for d in order:
        block = block + moved[d][:split].reshape(pairs, cols, shard).astype(F32)
        own = own + moved[d][split:].astype(F32)
    block_half = block.astype(BF16)
    total = block[0]
    for d in range(pairs - 1, 0, -1):
        total = total + over_resp(block_half[d], 2 * d).astype(F32)
    column = lax.dynamic_slice_in_dim(
        channel_scale, lax.axis_index("resp") * cols, cols
    )
    grad_prompt = (total * column[:, None]).T

    parts = own.reshape(-1, piece, 2 * rope)
    grad_span = jnp.concatenate(
        [parts[i] for i in range(latent // (2 * rope))] + [parts[-1][:, :rope]], axis=1
    )
    return (
        grad_latent.reshape(tok, heads, latent),
        grad_rope,
        grad_prompt,
        grad_span,
    )


def solution(mesh):
    return jax.shard_map(
        functools.partial(on_device, mesh.shape["resp"], mesh.shape["seq"]),
        mesh=mesh,
        in_specs=(
            P("seq", None),
            P(),
            P("resp", None),
            P("resp", "seq", None),
            P("resp", "seq"),
            P("resp", "seq", None),
            P(),
            P(),
            P(),
        ),
        out_specs=(
            P("resp", "seq", None),
            P("resp", "seq"),
            P("seq", "resp"),
            P(("resp", "seq"), None),
        ),
        check_vma=False,
    )
```

```python
import functools
import math

import jax
import jax.numpy as jnp
from jax import lax
from jax.experimental import pallas as pl
from jax.experimental.pallas import tpu as pltpu
from jax.sharding import PartitionSpec as P

SIGMA = 1.0 / math.sqrt(192.0)
EXP_SCALE = SIGMA * math.log2(math.e)
F32 = jnp.float32
BF16 = jnp.bfloat16
NT = (((1,), (1,)), ((), ()))
NN = (((1,), (0,)), ((), ()))
TN = (((0,), (0,)), ((), ()))
MIB = 1024 * 1024
STEP = 256


def dot(a, b, dims):
    return lax.dot_general(a, b, dims, preferred_element_type=F32)


def low_half(shape, half):
    return lax.broadcasted_iota(jnp.int32, shape, len(shape) - 1) < half


def put_keys(keys_ref, start, latent, values):
    rows, full = values.shape
    keys_ref[pl.ds(start, rows), :full] = values
    keys_ref[pl.ds(start, rows), full:] = values[:, latent:]


def scaled_rows(shard, scale):
    return (shard.astype(F32).T * scale).astype(BF16)


def mask_kernel(heads, mask_ref):
    key_pos = lax.broadcasted_iota(jnp.int32, mask_ref.shape, 0)
    row = lax.broadcasted_iota(jnp.int32, mask_ref.shape, 1)
    mask_ref[...] = jnp.where(key_pos * heads <= row, 1.0, 0.0)


def early_kernel(
    heads,
    length_s,
    response_s,
    index_s,
    mask_ref,
    scale_ref,
    prompt_ref,
    span_ref,
    q_ref,
    qrope_v,
    up_ref,
    qr_ref,
    expo_ref,
    dprob_ref,
    stat_ref,
    keys_ref,
    rope_scr,
):
    full, shard = prompt_ref.shape
    tok = span_ref.shape[0]
    rows, latent = q_ref.shape
    rope = full - latent
    my_resp = lax.axis_index("resp")
    live = jnp.clip(
        length_s[response_s[my_resp]] - index_s[my_resp] * tok, 0, tok
    )
    low = low_half((tok, 2 * rope), rope)
    for j in range(heads // 2):
        x = qrope_v[:, pl.ds(2 * rope * j, 2 * rope)].astype(F32)
        rope_scr[pl.ds(2 * j, tok, stride=heads), :] = jnp.where(low, x, 0.0)
        rope_scr[pl.ds(2 * j + 1, tok, stride=heads), :] = jnp.where(low, 0.0, x)
    qr_ref[...] = rope_scr[...].astype(BF16)

    put_keys(keys_ref, 0, latent, scaled_rows(prompt_ref[...], scale_ref[...]))
    put_keys(keys_ref, shard, latent, span_ref[...])

    for i in range(rows // STEP):
        at = pl.ds(i * STEP, STEP)
        logits = dot(keys_ref[:, :latent], q_ref[at, :], NT) + dot(
            keys_ref[:, latent:], qr_ref[at, :], NT
        )
        dprob = dot(keys_ref[:, :latent], up_ref[at, :], NT)
        key_pos = lax.broadcasted_iota(jnp.int32, (tok, STEP), 0)
        seen = (mask_ref[:, at] > 0.5) & (key_pos < live)
        own = jnp.where(seen, logits[shard:], -jnp.inf)
        logits = jnp.concatenate([logits[:shard], own], axis=0)
        top = jnp.max(logits, axis=0, keepdims=True)
        expo = jnp.exp2((logits - top) * EXP_SCALE)
        row_pos = (lax.broadcasted_iota(jnp.int32, (1, STEP), 1) + i * STEP) // heads
        expo_ref[:, at] = expo
        dprob_ref[:, at] = dprob
        stat_ref[0:1, at] = top
        stat_ref[1:2, at] = jnp.sum(expo, axis=0, keepdims=True)
        stat_ref[2:3, at] = jnp.sum(expo * dprob, axis=0, keepdims=True)
        stat_ref[3:4, at] = jnp.where(row_pos < live, SIGMA, 0.0)


def keys_kernel(
    n_resp,
    n_seq,
    scale_ref,
    q_ref,
    up_ref,
    qr_ref,
    expo_ref,
    dprob_ref,
    stat_ref,
    early_ref,
    *refs,
):
    shard_refs = refs[: n_seq - 1]
    mine_ref, theirs_ref, span_out, ds_ref, keys_ref, t_scr = refs[n_seq - 1 :]
    rows, latent = q_ref.shape
    full, shard = shard_refs[0].shape
    rope = full - latent
    prompt = shard * n_seq
    tok = early_ref.shape[0] - shard
    my_resp = lax.axis_index("resp")
    my_seq = lax.axis_index("seq")
    odd = (my_resp % 2) == 1

    scale = scale_ref[...]
    keys_ref[:shard] = early_ref[:shard]
    keys_ref[prompt:] = early_ref[shard:]
    for d in range(1, n_seq):
        value = shard_refs[d - 1][...]
        if d < n_seq - 1:
            other = shard_refs[(d - 1) ^ 1][...]
            value = jnp.where(odd, other, value)
        put_keys(keys_ref, d * shard, latent, scaled_rows(value, scale))

    late = slice(shard, prompt)
    for i in range(rows // STEP):
        at = pl.ds(i * STEP, STEP)
        logits = dot(keys_ref[late, :latent], q_ref[at, :], NT) + dot(
            keys_ref[late, latent:], qr_ref[at, :], NT
        )
        dprob = dot(keys_ref[late, :latent], up_ref[at, :], NT)
        early_top = stat_ref[0:1, at]
        top = jnp.maximum(early_top, jnp.max(logits, axis=0, keepdims=True))
        expo = jnp.exp2((logits - top) * EXP_SCALE)
        again = jnp.exp2((early_top - top) * EXP_SCALE)
        total = stat_ref[1:2, at] * again + jnp.sum(expo, axis=0, keepdims=True)
        weighed = stat_ref[2:3, at] * again + jnp.sum(expo * dprob, axis=0, keepdims=True)
        inverse = 1.0 / total
        delta = weighed * inverse
        factor = inverse * stat_ref[3:4, at]
        probs = expo * factor
        t_scr[late, at] = probs.astype(BF16)
        ds_ref[late, at] = (probs * (dprob - delta)).astype(BF16)
        probs = expo_ref[:, at] * (factor * again)
        dscore = probs * (dprob_ref[:, at] - delta)
        t_scr[:shard, at] = probs[:shard].astype(BF16)
        ds_ref[:shard, at] = dscore[:shard].astype(BF16)
        t_scr[prompt:, at] = probs[shard:].astype(BF16)
        ds_ref[prompt:, at] = dscore[shard:].astype(BF16)

    grad_latent = dot(ds_ref[...], q_ref[...], NN) + dot(t_scr[...], up_ref[...], NN) * (
        1.0 / SIGMA
    )
    grad_rope = dot(ds_ref[...], qr_ref[...], NN)

    piece = tok // n_seq
    own_rope = grad_rope[prompt:]
    own_rope = own_rope + pltpu.roll(own_rope, rope, 1)
    for s in range(n_seq):
        parts = [
            grad_latent[prompt + s * piece : prompt + (s + 1) * piece, c : c + 2 * rope]
            for c in range(0, latent, 2 * rope)
        ]
        parts.append(own_rope[s * piece : (s + 1) * piece])
        span_out[s ^ my_seq] = jnp.concatenate(parts, axis=0).astype(BF16)

    cols = full // n_resp
    my_pair = my_resp // 2
    scale_twice = jnp.concatenate([scale[:, latent:]] * 2, axis=1)
    for d in range(n_seq):
        at = slice(d * shard, (d + 1) * shard)
        lat = (grad_latent[at] * scale[:, :latent]).T
        rot = (grad_rope[at] * scale_twice).T
        whole = jnp.concatenate([lat, rot[:rope] + rot[rope:]], axis=0)
        for z in range(n_resp // 2):
            even_part = whole[2 * z * cols : (2 * z + 1) * cols]
            odd_part = whole[(2 * z + 1) * cols : (2 * z + 2) * cols]
            mine_ref[d, z ^ my_pair] = jnp.where(odd, odd_part, even_part).astype(BF16)
            theirs_ref[d, z ^ my_pair] = jnp.where(odd, even_part, odd_part).astype(BF16)


def query_kernel(heads, first, count, ds_ref, keys_ref, *refs):
    out_hbm, rope_hbm, out_v, rope_v, rope_scr, out_sems, rope_sems = refs[-7:]
    latent = out_v.shape[1]
    rope = (keys_ref.shape[1] - latent) // 2
    step = 16 * heads
    low = low_half((16, 2 * rope), rope)
    copies = []
    for i in range(count):
        at = pl.ds((first + i) * step, step)
        here = pl.ds(i * step, step)
        out_v[here, :] = dot(ds_ref[:, at], keys_ref[:, :latent], TN).astype(BF16)
        copies.append(pltpu.make_async_copy(out_v.at[here], out_hbm.at[at], out_sems.at[i]))
        copies[-1].start()
        rope_scr[...] = dot(ds_ref[:, at], keys_ref[:, latent:], TN)
        for j in range(heads // 2):
            even = rope_scr[pl.ds(2 * j, 16, stride=heads), :]
            odd = rope_scr[pl.ds(2 * j + 1, 16, stride=heads), :]
            rope_v[pl.ds(i * 16, 16), pl.ds(2 * rope * j, 2 * rope)] = jnp.where(
                low, even, odd
            ).astype(BF16)
        copies.append(
            pltpu.make_async_copy(
                rope_v.at[pl.ds(i * 16, 16)],
                rope_hbm.at[pl.ds((first + i) * 16, 16)],
                rope_sems.at[i],
            )
        )
        copies[-1].start()
    for copy in copies:
        copy.wait()


def on_device(
    n_resp,
    n_seq,
    prompt_cache,
    channel_scale,
    span_cache,
    q_latent,
    q_rope,
    d_out,
    resp_length,
    span_response,
    span_index,
):
    tok, heads, latent = q_latent.shape
    shard, full = prompt_cache.shape
    rope = full - latent
    rows = tok * heads
    prompt = shard * n_seq
    keys = prompt + tok
    early = shard + tok
    width = latent + 2 * rope
    cols = full // n_resp
    pairs = n_resp // 2
    piece = tok // n_seq
    span_rows = piece * (latent // (2 * rope) + 1)
    vmem = pl.BlockSpec(memory_space=pltpu.VMEM)
    hbm = pl.BlockSpec(memory_space=pl.ANY)

    def shape(dims, dtype=BF16):
        return jax.ShapeDtypeStruct(dims, dtype)

    def over_seq(x, d):
        return lax.ppermute(x, "seq", [(i, i ^ d) for i in range(n_seq)])

    def over_resp(x, d):
        return lax.ppermute(x, "resp", [(i, i ^ d) for i in range(n_resp)])

    def by_core(x, d):
        moves = [
            (r * n_seq + s, r * n_seq + (s ^ (d + r % 2)))
            for r in range(n_resp)
            for s in range(n_seq)
        ]
        return lax.ppermute(x, ("resp", "seq"), moves)

    prompt_t = prompt_cache.T
    fetched = [by_core(prompt_t, d) for d in range(1, n_seq - 1, 2)]
    last = over_seq(prompt_t, n_seq - 1)

    scale_row = channel_scale.reshape(1, full)
    smem = pl.BlockSpec(memory_space=pltpu.SMEM)
    q_rows = q_latent.reshape(rows, latent)
    up_rows = d_out.reshape(rows, latent)
    mask = pl.pallas_call(
        functools.partial(mask_kernel, heads),
        out_shape=shape((tok, rows), F32),
        out_specs=vmem,
        compiler_params=pltpu.CompilerParams(vmem_limit_bytes=4 * MIB),
        cost_estimate=pl.CostEstimate(
            flops=40 * keys * rows * width, bytes_accessed=4 * tok * rows, transcendentals=0
        ),
        name="mask",
    )()
    q_turned, expo, dprob, stats, early_keys = pl.pallas_call(
        functools.partial(early_kernel, heads),
        out_shape=(
            shape((rows, 2 * rope)),
            shape((early, rows), F32),
            shape((early, rows), F32),
            shape((8, rows), F32),
            shape((early, width)),
        ),
        in_specs=[smem] * 3 + [vmem] * 7,
        out_specs=(vmem,) * 5,
        scratch_shapes=[pltpu.VMEM((rows, 2 * rope), F32)],
        compiler_params=pltpu.CompilerParams(vmem_limit_bytes=24 * MIB),
        cost_estimate=pl.CostEstimate(
            flops=2 * early * rows * 2 * latent, bytes_accessed=4 * rows * latent, transcendentals=0
        ),
        name="early",
    )(
        resp_length,
        span_response,
        span_index,
        mask,
        scale_row,
        prompt_t,
        span_cache,
        q_rows,
        q_rope,
        up_rows,
    )

    fetched, stats = lax.optimization_barrier((fetched, stats))
    shards = []
    for value in fetched:
        shards += [value, over_resp(value, 1)]
    shards.append(last)
    mine, theirs, span, dscore, keys_all = pl.pallas_call(
        functools.partial(keys_kernel, n_resp, n_seq),
        out_shape=(
            shape((n_seq, pairs, cols, shard)),
            shape((n_seq, pairs, cols, shard)),
            shape((n_seq, span_rows, 2 * rope)),
            shape((keys, rows)),
            shape((keys, width)),
        ),
        in_specs=[vmem] * (7 + n_seq),
        out_specs=(vmem,) * 5,
        scratch_shapes=[pltpu.VMEM((keys, rows), BF16)],
        compiler_params=pltpu.CompilerParams(vmem_limit_bytes=24 * MIB),
        cost_estimate=pl.CostEstimate(
            flops=2 * keys * rows * 3 * latent, bytes_accessed=4 * rows * latent, transcendentals=0
        ),
        name="keys",
    )(scale_row, q_rows, up_rows, q_turned, expo, dprob, stats, early_keys, *shards)

    steps = tok // 16

    def queries(first, count, dscore, keys_all, before):
        return pl.pallas_call(
            functools.partial(query_kernel, heads, first, count),
            out_shape=(shape((rows, latent)), shape((tok, heads * rope))),
            in_specs=[vmem] * 2 + [hbm] * len(before),
            out_specs=(hbm,) * 2,
            scratch_shapes=[
                pltpu.VMEM((count * 16 * heads, latent), BF16),
                pltpu.VMEM((count * 16, heads * rope), BF16),
                pltpu.VMEM((16 * heads, 2 * rope), F32),
                pltpu.SemaphoreType.DMA((count,)),
                pltpu.SemaphoreType.DMA((count,)),
            ],
            input_output_aliases={2: 0, 3: 1} if before else {},
            compiler_params=pltpu.CompilerParams(vmem_limit_bytes=16 * MIB),
            cost_estimate=pl.CostEstimate(
                flops=2 * keys * count * 16 * heads * width,
                bytes_accessed=count * 32 * heads * latent,
                transcendentals=0,
            ),
            name="queries",
        )(dscore, keys_all, *before)

    summed = mine.astype(F32) + over_resp(theirs, 1).astype(F32)
    held = summed.astype(BF16).reshape(n_seq, pairs * cols, shard)
    moved = {
        d: over_seq(jnp.concatenate([held[d].reshape(-1, 2 * rope), span[d]], axis=0), d)
        for d in range(n_seq - 1, 0, -1)
    }
    half = (steps + 1) // 2
    partly = queries(0, half, dscore, keys_all, ())
    split = pairs * cols * shard // (2 * rope)
    block = summed[0].reshape(pairs, cols, shard)
    own = span[0].astype(F32)
    for d in moved:
        block = block + moved[d][:split].reshape(pairs, cols, shard).astype(F32)
        own = own + moved[d][split:].astype(F32)
    block_half = block.astype(BF16)
    block_half, dscore, keys_all = lax.optimization_barrier((block_half, dscore, keys_all))
    arrived = [over_resp(block_half[d], 2 * d) for d in range(pairs - 1, 0, -1)]
    grad_latent, grad_rope = queries(half, steps - half, dscore, keys_all, partly)
    total = block[0]
    for x in arrived:
        total = total + x.astype(F32)
    grad_prompt = total.T

    parts = own.reshape(-1, piece, 2 * rope)
    grad_span = jnp.concatenate(
        [parts[i] for i in range(latent // (2 * rope))] + [parts[-1][:, :rope]], axis=1
    )
    return (
        grad_latent.reshape(tok, heads, latent),
        grad_rope,
        grad_prompt,
        grad_span,
    )


def solution(mesh):
    return jax.shard_map(
        functools.partial(on_device, mesh.shape["resp"], mesh.shape["seq"]),
        mesh=mesh,
        in_specs=(
            P("seq", None),
            P(),
            P("resp", None),
            P("resp", "seq", None),
            P("resp", "seq"),
            P("resp", "seq", None),
            P(),
            P(),
            P(),
        ),
        out_specs=(
            P("resp", "seq", None),
            P("resp", "seq"),
            P("seq", "resp"),
            P(("resp", "seq"), None),
        ),
        check_vma=False,
    )
```

```python
import functools
import math

import jax
import jax.numpy as jnp
from jax import lax
from jax.experimental import pallas as pl
from jax.experimental.pallas import tpu as pltpu
from jax.sharding import PartitionSpec as P

SIGMA = 1.0 / math.sqrt(192.0)
EXP_SCALE = SIGMA * math.log2(math.e)
F32 = jnp.float32
BF16 = jnp.bfloat16
NT = (((1,), (1,)), ((), ()))
NN = (((1,), (0,)), ((), ()))
TN = (((0,), (0,)), ((), ()))
MIB = 1024 * 1024
STEP = 256


def dot(a, b, dims):
    return lax.dot_general(a, b, dims, preferred_element_type=F32)


def low_half(shape, half):
    return lax.broadcasted_iota(jnp.int32, shape, len(shape) - 1) < half


def put_keys(keys_ref, start, latent, values):
    rows, full = values.shape
    keys_ref[pl.ds(start, rows), :full] = values
    keys_ref[pl.ds(start, rows), full:] = values[:, latent:]


def scaled_rows(shard, scale):
    return (shard.astype(F32).T * scale).astype(BF16)


def mask_kernel(heads, mask_ref):
    key_pos = lax.broadcasted_iota(jnp.int32, mask_ref.shape, 0)
    row = lax.broadcasted_iota(jnp.int32, mask_ref.shape, 1)
    mask_ref[...] = jnp.where(key_pos * heads <= row, 1.0, 0.0)


def partial_softmax(keys_ref, at, q_ref, qr_ref, up_ref):
    latent = q_ref.shape[1]
    logits = dot(keys_ref[:, :latent], q_ref[at, :], NT) + dot(
        keys_ref[:, latent:], qr_ref[at, :], NT
    )
    return logits, dot(keys_ref[:, :latent], up_ref[at, :], NT) * SIGMA


def early_kernel(
    heads,
    length_s,
    response_s,
    index_s,
    mask_ref,
    scale_ref,
    prompt_ref,
    span_ref,
    q_ref,
    qrope_v,
    up_ref,
    qr_ref,
    expo_ref,
    dprob_ref,
    stat_ref,
    keys_ref,
    rope_scr,
):
    full, shard = prompt_ref.shape
    tok = span_ref.shape[0]
    rows, latent = q_ref.shape
    rope = full - latent
    my_resp = lax.axis_index("resp")
    live = jnp.clip(
        length_s[response_s[my_resp]] - index_s[my_resp] * tok, 0, tok
    )
    low = low_half((tok, 2 * rope), rope)
    for j in range(heads // 2):
        x = qrope_v[:, pl.ds(2 * rope * j, 2 * rope)].astype(F32)
        rope_scr[pl.ds(2 * j, tok, stride=heads), :] = jnp.where(low, x, 0.0)
        rope_scr[pl.ds(2 * j + 1, tok, stride=heads), :] = jnp.where(low, 0.0, x)
    qr_ref[...] = rope_scr[...].astype(BF16)

    put_keys(keys_ref, 0, latent, scaled_rows(prompt_ref[...], scale_ref[...]))
    put_keys(keys_ref, shard, latent, span_ref[...])

    for i in range(rows // STEP):
        at = pl.ds(i * STEP, STEP)
        logits, dprob = partial_softmax(keys_ref, at, q_ref, qr_ref, up_ref)
        key_pos = lax.broadcasted_iota(jnp.int32, (tok, STEP), 0)
        seen = (mask_ref[:, at] > 0.5) & (key_pos < live)
        own = jnp.where(seen, logits[shard:], -jnp.inf)
        logits = jnp.concatenate([logits[:shard], own], axis=0)
        top = jnp.max(logits, axis=0, keepdims=True)
        expo = jnp.exp2((logits - top) * EXP_SCALE)
        row_pos = (lax.broadcasted_iota(jnp.int32, (1, STEP), 1) + i * STEP) // heads
        expo_ref[:, at] = expo
        dprob_ref[:, at] = dprob
        stat_ref[0:1, at] = top
        stat_ref[1:2, at] = jnp.sum(expo, axis=0, keepdims=True)
        stat_ref[2:3, at] = jnp.sum(expo * dprob, axis=0, keepdims=True)
        stat_ref[3:4, at] = jnp.where(row_pos < live, 1.0, 0.0)


def middle_kernel(scale_ref, q_ref, up_ref, qr_ref, stat_ref, *refs):
    shard_refs = refs[:-4]
    expo_ref, dprob_ref, out_ref, keys_ref = refs[-4:]
    rows, latent = q_ref.shape
    shard = shard_refs[0].shape[1]
    for d, ref in enumerate(shard_refs):
        put_keys(keys_ref, d * shard, latent, scaled_rows(ref[...], scale_ref[...]))
    for i in range(rows // STEP):
        at = pl.ds(i * STEP, STEP)
        logits, dprob = partial_softmax(keys_ref, at, q_ref, qr_ref, up_ref)
        before = stat_ref[0:1, at]
        top = jnp.maximum(before, jnp.max(logits, axis=0, keepdims=True))
        expo = jnp.exp2((logits - top) * EXP_SCALE)
        again = jnp.exp2((before - top) * EXP_SCALE)
        expo_ref[:, at] = expo
        dprob_ref[:, at] = dprob
        out_ref[0:1, at] = top
        out_ref[1:2, at] = stat_ref[1:2, at] * again + jnp.sum(expo, axis=0, keepdims=True)
        out_ref[2:3, at] = stat_ref[2:3, at] * again + jnp.sum(
            expo * dprob, axis=0, keepdims=True
        )
        out_ref[3:4, at] = stat_ref[3:4, at]
        out_ref[4:5, at] = before


def keys_kernel(
    n_resp,
    n_seq,
    scale_ref,
    q_ref,
    up_ref,
    qr_ref,
    expo_a,
    dprob_a,
    keys_a,
    expo_b,
    dprob_b,
    keys_b,
    stat_ref,
    *refs,
):
    shard_refs = refs[:-7]
    mine_ref, theirs_ref, span_out, ds_ref, keys_ref, p_scr, keys_c = refs[-7:]
    rows, latent = q_ref.shape
    full = scale_ref.shape[1]
    shard = shard_refs[0].shape[1]
    rope = full - latent
    prompt = shard * n_seq
    tok = keys_a.shape[0] - shard
    my_resp = lax.axis_index("resp")
    my_seq = lax.axis_index("seq")
    odd = (my_resp % 2) == 1

    middle = slice(shard, shard + keys_b.shape[0])
    late = slice(middle.stop, prompt)
    scale = scale_ref[...]
    for d, ref in enumerate(shard_refs):
        put_keys(keys_c, d * shard, latent, scaled_rows(ref[...], scale))
    keys_ref[:shard] = keys_a[:shard]
    keys_ref[middle] = keys_b[...]
    keys_ref[late] = keys_c[...]
    keys_ref[prompt:] = keys_a[shard:]

    for i in range(rows // STEP):
        at = pl.ds(i * STEP, STEP)
        logits, dprob = partial_softmax(keys_c, at, q_ref, qr_ref, up_ref)
        before = stat_ref[0:1, at]
        top = jnp.maximum(before, jnp.max(logits, axis=0, keepdims=True))
        expo = jnp.exp2((logits - top) * EXP_SCALE)
        again = jnp.exp2((before - top) * EXP_SCALE)
        total = stat_ref[1:2, at] * again + jnp.sum(expo, axis=0, keepdims=True)
        weighed = stat_ref[2:3, at] * again + jnp.sum(expo * dprob, axis=0, keepdims=True)
        inverse = 1.0 / total
        delta = weighed * inverse
        factor = inverse * stat_ref[3:4, at]
        probs = expo * factor
        p_scr[late, at] = probs.astype(BF16)
        ds_ref[late, at] = (probs * (dprob - delta)).astype(BF16)
        probs = expo_b[:, at] * (factor * again)
        p_scr[middle, at] = probs.astype(BF16)
        ds_ref[middle, at] = (probs * (dprob_b[:, at] - delta)).astype(BF16)
        first = jnp.exp2((stat_ref[4:5, at] - top) * EXP_SCALE)
        probs = expo_a[:, at] * (factor * first)
        dscore = probs * (dprob_a[:, at] - delta)
        p_scr[:shard, at] = probs[:shard].astype(BF16)
        ds_ref[:shard, at] = dscore[:shard].astype(BF16)
        p_scr[prompt:, at] = probs[shard:].astype(BF16)
        ds_ref[prompt:, at] = dscore[shard:].astype(BF16)

    grad_latent = dot(ds_ref[...], q_ref[...], NN) + dot(p_scr[...], up_ref[...], NN)
    grad_rope = dot(ds_ref[...], qr_ref[...], NN)

    piece = tok // n_seq
    own_rope = grad_rope[prompt:]
    own_rope = own_rope + pltpu.roll(own_rope, rope, 1)
    for s in range(n_seq):
        parts = [
            grad_latent[prompt + s * piece : prompt + (s + 1) * piece, c : c + 2 * rope]
            for c in range(0, latent, 2 * rope)
        ]
        parts.append(own_rope[s * piece : (s + 1) * piece])
        span_out[s ^ my_seq] = jnp.concatenate(parts, axis=0).astype(BF16)

    cols = full // n_resp
    my_pair = my_resp // 2
    scale_twice = jnp.concatenate([scale[:, latent:]] * 2, axis=1)
    pairs = n_seq // 2 - 1
    for slot in range(n_seq):
        at = slice(slot * shard, (slot + 1) * shard)
        lat = (grad_latent[at] * scale[:, :latent]).T
        rot = (grad_rope[at] * scale_twice).T
        whole = jnp.concatenate([lat, rot[:rope] + rot[rope:]], axis=0)
        for z in range(n_resp // 2):
            even_part = whole[2 * z * cols : (2 * z + 1) * cols]
            odd_part = whole[(2 * z + 1) * cols : (2 * z + 2) * cols]
            mine = jnp.where(odd, odd_part, even_part).astype(BF16)
            theirs = jnp.where(odd, even_part, odd_part).astype(BF16)
            if slot in (0, n_seq - 1):
                d = slot
            elif slot <= pairs:
                d = 2 * slot - 1 + my_resp % 2
            else:
                d = 2 * (slot - pairs) - my_resp % 2
            mine_ref[d, z ^ my_pair] = mine
            theirs_ref[d, z ^ my_pair] = theirs


def query_kernel(heads, first, count, ds_ref, keys_ref, *refs):
    out_hbm, rope_hbm, out_v, rope_v, rope_scr, out_sems, rope_sems = refs[-7:]
    latent = out_v.shape[1]
    rope = (keys_ref.shape[1] - latent) // 2
    step = 16 * heads
    low = low_half((16, 2 * rope), rope)
    copies = []
    for i in range(count):
        at = pl.ds((first + i) * step, step)
        here = pl.ds(i * step, step)
        out_v[here, :] = dot(ds_ref[:, at], keys_ref[:, :latent], TN).astype(BF16)
        copies.append(pltpu.make_async_copy(out_v.at[here], out_hbm.at[at], out_sems.at[i]))
        copies[-1].start()
        rope_scr[...] = dot(ds_ref[:, at], keys_ref[:, latent:], TN)
        for j in range(heads // 2):
            even = rope_scr[pl.ds(2 * j, 16, stride=heads), :]
            odd = rope_scr[pl.ds(2 * j + 1, 16, stride=heads), :]
            rope_v[pl.ds(i * 16, 16), pl.ds(2 * rope * j, 2 * rope)] = jnp.where(
                low, even, odd
            ).astype(BF16)
        copies.append(
            pltpu.make_async_copy(
                rope_v.at[pl.ds(i * 16, 16)],
                rope_hbm.at[pl.ds((first + i) * 16, 16)],
                rope_sems.at[i],
            )
        )
        copies[-1].start()
    for copy in copies:
        copy.wait()


def on_device(
    n_resp,
    n_seq,
    prompt_cache,
    channel_scale,
    span_cache,
    q_latent,
    q_rope,
    d_out,
    resp_length,
    span_response,
    span_index,
):
    tok, heads, latent = q_latent.shape
    shard, full = prompt_cache.shape
    rope = full - latent
    rows = tok * heads
    prompt = shard * n_seq
    keys = prompt + tok
    early = shard + tok
    width = latent + 2 * rope
    cols = full // n_resp
    pairs = n_resp // 2
    piece = tok // n_seq
    span_rows = piece * (latent // (2 * rope) + 1)
    vmem = pl.BlockSpec(memory_space=pltpu.VMEM)
    hbm = pl.BlockSpec(memory_space=pl.ANY)

    def shape(dims, dtype=BF16):
        return jax.ShapeDtypeStruct(dims, dtype)

    def over_seq(x, d):
        return lax.ppermute(x, "seq", [(i, i ^ d) for i in range(n_seq)])

    def over_resp(x, d):
        return lax.ppermute(x, "resp", [(i, i ^ d) for i in range(n_resp)])

    def by_core(x, d):
        moves = [
            (r * n_seq + s, r * n_seq + (s ^ (d + r % 2)))
            for r in range(n_resp)
            for s in range(n_seq)
        ]
        return lax.ppermute(x, ("resp", "seq"), moves)

    prompt_t = prompt_cache.T
    fetched = [by_core(prompt_t, d) for d in range(1, n_seq - 1, 2)]

    scale_row = channel_scale.reshape(1, full)
    smem = pl.BlockSpec(memory_space=pltpu.SMEM)
    q_rows = q_latent.reshape(rows, latent)
    up_rows = d_out.reshape(rows, latent)
    mask = pl.pallas_call(
        functools.partial(mask_kernel, heads),
        out_shape=shape((tok, rows), F32),
        out_specs=vmem,
        compiler_params=pltpu.CompilerParams(vmem_limit_bytes=4 * MIB),
        cost_estimate=pl.CostEstimate(
            flops=40 * keys * rows * width, bytes_accessed=4 * tok * rows, transcendentals=0
        ),
        name="mask",
    )()
    again, mask = lax.optimization_barrier((prompt_t, mask))
    last = over_seq(again, n_seq - 1)
    q_turned, expo, dprob, stats, early_keys = pl.pallas_call(
        functools.partial(early_kernel, heads),
        out_shape=(
            shape((rows, 2 * rope)),
            shape((early, rows), F32),
            shape((early, rows), F32),
            shape((8, rows), F32),
            shape((early, width)),
        ),
        in_specs=[smem] * 3 + [vmem] * 7,
        out_specs=(vmem,) * 5,
        scratch_shapes=[pltpu.VMEM((rows, 2 * rope), F32)],
        compiler_params=pltpu.CompilerParams(vmem_limit_bytes=24 * MIB),
        cost_estimate=pl.CostEstimate(
            flops=2 * early * rows * 2 * latent, bytes_accessed=4 * rows * latent, transcendentals=0
        ),
        name="early",
    )(
        resp_length,
        span_response,
        span_index,
        mask,
        scale_row,
        prompt_t,
        span_cache,
        q_rows,
        q_rope,
        up_rows,
    )

    fetched, stats = lax.optimization_barrier((fetched, stats))
    swapped = [over_resp(value, 1) for value in fetched]
    middle = shard * len(fetched)
    expo_b, dprob_b, stats, middle_keys = pl.pallas_call(
        middle_kernel,
        out_shape=(
            shape((middle, rows), F32),
            shape((middle, rows), F32),
            shape((8, rows), F32),
            shape((middle, width)),
        ),
        in_specs=[vmem] * (5 + len(fetched)),
        out_specs=(vmem,) * 4,
        compiler_params=pltpu.CompilerParams(vmem_limit_bytes=24 * MIB),
        cost_estimate=pl.CostEstimate(
            flops=2 * middle * rows * 2 * latent, bytes_accessed=4 * rows * latent, transcendentals=0
        ),
        name="middle",
    )(scale_row, q_rows, up_rows, q_turned, stats, *fetched)

    mine, theirs, span, dscore, keys_all = pl.pallas_call(
        functools.partial(keys_kernel, n_resp, n_seq),
        out_shape=(
            shape((n_seq, pairs, cols, shard)),
            shape((n_seq, pairs, cols, shard)),
            shape((n_seq, span_rows, 2 * rope)),
            shape((keys, rows)),
            shape((keys, width)),
        ),
        in_specs=[vmem] * (12 + len(swapped)),
        out_specs=(vmem,) * 5,
        scratch_shapes=[
            pltpu.VMEM((keys, rows), BF16),
            pltpu.VMEM((shard * (len(swapped) + 1), width), BF16),
        ],
        compiler_params=pltpu.CompilerParams(vmem_limit_bytes=24 * MIB),
        cost_estimate=pl.CostEstimate(
            flops=2 * keys * rows * 3 * latent, bytes_accessed=4 * rows * latent, transcendentals=0
        ),
        name="keys",
    )(
        scale_row,
        q_rows,
        up_rows,
        q_turned,
        expo,
        dprob,
        early_keys,
        expo_b,
        dprob_b,
        middle_keys,
        stats,
        *swapped,
        last,
    )

    steps = tok // 16

    def queries(first, count, dscore, keys_all, before):
        return pl.pallas_call(
            functools.partial(query_kernel, heads, first, count),
            out_shape=(shape((rows, latent)), shape((tok, heads * rope))),
            in_specs=[vmem] * 2 + [hbm] * len(before),
            out_specs=(hbm,) * 2,
            scratch_shapes=[
                pltpu.VMEM((count * 16 * heads, latent), BF16),
                pltpu.VMEM((count * 16, heads * rope), BF16),
                pltpu.VMEM((16 * heads, 2 * rope), F32),
                pltpu.SemaphoreType.DMA((count,)),
                pltpu.SemaphoreType.DMA((count,)),
            ],
            input_output_aliases={2: 0, 3: 1} if before else {},
            compiler_params=pltpu.CompilerParams(vmem_limit_bytes=16 * MIB),
            cost_estimate=pl.CostEstimate(
                flops=2 * keys * count * 16 * heads * width,
                bytes_accessed=count * 32 * heads * latent,
                transcendentals=0,
            ),
            name="queries",
        )(dscore, keys_all, *before)

    summed = mine.astype(F32) + over_resp(theirs, 1).astype(F32)
    held = summed.astype(BF16).reshape(n_seq, pairs * cols, shard)
    moved = {
        d: over_seq(jnp.concatenate([held[d].reshape(-1, 2 * rope), span[d]], axis=0), d)
        for d in range(n_seq - 1, 0, -1)
    }
    half = (3 * steps + 3) // 4
    partly = queries(0, half, dscore, keys_all, ())
    split = pairs * cols * shard // (2 * rope)
    block = summed[0].reshape(pairs, cols, shard)
    own = span[0].astype(F32)
    for d in moved:
        block = block + moved[d][:split].reshape(pairs, cols, shard).astype(F32)
        own = own + moved[d][split:].astype(F32)
    block_half = block.astype(BF16)
    block_half, dscore, keys_all = lax.optimization_barrier((block_half, dscore, keys_all))
    arrived = [over_resp(block_half[d], 2 * d) for d in range(pairs - 1, 0, -1)]
    grad_latent, grad_rope = queries(half, steps - half, dscore, keys_all, partly)
    total = block[0]
    for x in arrived:
        total = total + x.astype(F32)
    grad_prompt = total.T

    parts = own.reshape(-1, piece, 2 * rope)
    grad_span = jnp.concatenate(
        [parts[i] for i in range(latent // (2 * rope))] + [parts[-1][:, :rope]], axis=1
    )
    return (
        grad_latent.reshape(tok, heads, latent),
        grad_rope,
        grad_prompt,
        grad_span,
    )


def solution(mesh):
    return jax.shard_map(
        functools.partial(on_device, mesh.shape["resp"], mesh.shape["seq"]),
        mesh=mesh,
        in_specs=(
            P("seq", None),
            P(),
            P("resp", None),
            P("resp", "seq", None),
            P("resp", "seq"),
            P("resp", "seq", None),
            P(),
            P(),
            P(),
        ),
        out_specs=(
            P("resp", "seq", None),
            P("resp", "seq"),
            P("seq", "resp"),
            P(("resp", "seq"), None),
        ),
        check_vma=False,
    )
```

```python
import functools
import math

import jax
import jax.numpy as jnp
from jax import lax
from jax.experimental import pallas as pl
from jax.experimental.pallas import tpu as pltpu
from jax.sharding import PartitionSpec as P

SIGMA = 1.0 / math.sqrt(192.0)
EXP_SCALE = SIGMA * math.log2(math.e)
F32 = jnp.float32
BF16 = jnp.bfloat16
NT = (((1,), (1,)), ((), ()))
NN = (((1,), (0,)), ((), ()))
TN = (((0,), (0,)), ((), ()))
MIB = 1024 * 1024
STEP = 256


def dot(a, b, dims):
    return lax.dot_general(a, b, dims, preferred_element_type=F32)


def low_half(shape, half):
    return lax.broadcasted_iota(jnp.int32, shape, len(shape) - 1) < half


def put_keys(keys_ref, start, latent, values):
    rows, full = values.shape
    keys_ref[pl.ds(start, rows), :full] = values
    keys_ref[pl.ds(start, rows), full:] = values[:, latent:]


def scaled_rows(shard, scale):
    return (shard.astype(F32).T * scale).astype(BF16)


def mask_kernel(heads, mask_ref):
    key_pos = lax.broadcasted_iota(jnp.int32, mask_ref.shape, 0)
    row = lax.broadcasted_iota(jnp.int32, mask_ref.shape, 1)
    mask_ref[...] = jnp.where(key_pos * heads <= row, 1.0, 0.0)


def partial_softmax(keys_ref, at, q_ref, qr_ref, up_ref):
    latent = q_ref.shape[1]
    logits = dot(keys_ref[:, :latent], q_ref[at, :], NT) + dot(
        keys_ref[:, latent:], qr_ref[at, :], NT
    )
    return logits, dot(keys_ref[:, :latent], up_ref[at, :], NT) * SIGMA


def early_kernel(
    heads,
    length_s,
    response_s,
    index_s,
    mask_ref,
    scale_ref,
    prompt_ref,
    span_ref,
    q_ref,
    qrope_v,
    up_ref,
    qr_ref,
    expo_ref,
    dprob_ref,
    stat_ref,
    keys_ref,
    rope_scr,
):
    full, shard = prompt_ref.shape
    tok = span_ref.shape[0]
    rows, latent = q_ref.shape
    rope = full - latent
    my_resp = lax.axis_index("resp")
    live = jnp.clip(
        length_s[response_s[my_resp]] - index_s[my_resp] * tok, 0, tok
    )
    low = low_half((tok, 2 * rope), rope)
    for j in range(heads // 2):
        x = qrope_v[:, pl.ds(2 * rope * j, 2 * rope)].astype(F32)
        rope_scr[pl.ds(2 * j, tok, stride=heads), :] = jnp.where(low, x, 0.0)
        rope_scr[pl.ds(2 * j + 1, tok, stride=heads), :] = jnp.where(low, 0.0, x)
    qr_ref[...] = rope_scr[...].astype(BF16)

    put_keys(keys_ref, 0, latent, scaled_rows(prompt_ref[...], scale_ref[...]))
    put_keys(keys_ref, shard, latent, span_ref[...])

    for i in range(rows // STEP):
        at = pl.ds(i * STEP, STEP)
        logits, dprob = partial_softmax(keys_ref, at, q_ref, qr_ref, up_ref)
        key_pos = lax.broadcasted_iota(jnp.int32, (tok, STEP), 0)
        seen = (mask_ref[:, at] > 0.5) & (key_pos < live)
        own = jnp.where(seen, logits[shard:], -jnp.inf)
        logits = jnp.concatenate([logits[:shard], own], axis=0)
        top = jnp.max(logits, axis=0, keepdims=True)
        expo = jnp.exp2((logits - top) * EXP_SCALE)
        row_pos = (lax.broadcasted_iota(jnp.int32, (1, STEP), 1) + i * STEP) // heads
        expo_ref[:, at] = expo
        dprob_ref[:, at] = dprob
        stat_ref[0:1, at] = top
        stat_ref[1:2, at] = jnp.sum(expo, axis=0, keepdims=True)
        stat_ref[2:3, at] = jnp.sum(expo * dprob, axis=0, keepdims=True)
        stat_ref[3:4, at] = jnp.where(row_pos < live, 1.0, 0.0)


def middle_kernel(scale_ref, q_ref, up_ref, qr_ref, stat_ref, *refs):
    shard_refs = refs[:-4]
    expo_ref, dprob_ref, out_ref, keys_ref = refs[-4:]
    rows, latent = q_ref.shape
    shard = shard_refs[0].shape[1]
    for d, ref in enumerate(shard_refs):
        put_keys(keys_ref, d * shard, latent, scaled_rows(ref[...], scale_ref[...]))
    for i in range(rows // STEP):
        at = pl.ds(i * STEP, STEP)
        logits, dprob = partial_softmax(keys_ref, at, q_ref, qr_ref, up_ref)
        before = stat_ref[0:1, at]
        top = jnp.maximum(before, jnp.max(logits, axis=0, keepdims=True))
        expo = jnp.exp2((logits - top) * EXP_SCALE)
        again = jnp.exp2((before - top) * EXP_SCALE)
        expo_ref[:, at] = expo
        dprob_ref[:, at] = dprob
        out_ref[0:1, at] = top
        out_ref[1:2, at] = stat_ref[1:2, at] * again + jnp.sum(expo, axis=0, keepdims=True)
        out_ref[2:3, at] = stat_ref[2:3, at] * again + jnp.sum(
            expo * dprob, axis=0, keepdims=True
        )
        out_ref[3:4, at] = stat_ref[3:4, at]
        out_ref[4:5, at] = before


def keys_kernel(
    n_resp,
    n_seq,
    scale_ref,
    q_ref,
    up_ref,
    qr_ref,
    expo_a,
    dprob_a,
    keys_a,
    expo_b,
    dprob_b,
    keys_b,
    stat_ref,
    *refs,
):
    shard_refs = refs[:-7]
    mine_ref, theirs_ref, span_out, ds_ref, keys_ref, p_scr, keys_c = refs[-7:]
    rows, latent = q_ref.shape
    full = scale_ref.shape[1]
    shard = shard_refs[0].shape[1]
    rope = full - latent
    prompt = shard * n_seq
    tok = keys_a.shape[0] - shard
    my_resp = lax.axis_index("resp")
    my_seq = lax.axis_index("seq")
    odd = (my_resp % 2) == 1

    middle = slice(shard, shard + keys_b.shape[0])
    late = slice(middle.stop, prompt)
    scale = scale_ref[...]
    for d, ref in enumerate(shard_refs):
        put_keys(keys_c, d * shard, latent, scaled_rows(ref[...], scale))
    keys_ref[:shard] = keys_a[:shard]
    keys_ref[middle] = keys_b[...]
    keys_ref[late] = keys_c[...]
    keys_ref[prompt:] = keys_a[shard:]

    for i in range(rows // STEP):
        at = pl.ds(i * STEP, STEP)
        logits, dprob = partial_softmax(keys_c, at, q_ref, qr_ref, up_ref)
        before = stat_ref[0:1, at]
        top = jnp.maximum(before, jnp.max(logits, axis=0, keepdims=True))
        expo = jnp.exp2((logits - top) * EXP_SCALE)
        again = jnp.exp2((before - top) * EXP_SCALE)
        total = stat_ref[1:2, at] * again + jnp.sum(expo, axis=0, keepdims=True)
        weighed = stat_ref[2:3, at] * again + jnp.sum(expo * dprob, axis=0, keepdims=True)
        inverse = 1.0 / total
        delta = weighed * inverse
        factor = inverse * stat_ref[3:4, at]
        probs = expo * factor
        p_scr[late, at] = probs.astype(BF16)
        ds_ref[late, at] = (probs * (dprob - delta)).astype(BF16)
        probs = expo_b[:, at] * (factor * again)
        p_scr[middle, at] = probs.astype(BF16)
        ds_ref[middle, at] = (probs * (dprob_b[:, at] - delta)).astype(BF16)
        first = jnp.exp2((stat_ref[4:5, at] - top) * EXP_SCALE)
        probs = expo_a[:, at] * (factor * first)
        dscore = probs * (dprob_a[:, at] - delta)
        p_scr[:shard, at] = probs[:shard].astype(BF16)
        ds_ref[:shard, at] = dscore[:shard].astype(BF16)
        p_scr[prompt:, at] = probs[shard:].astype(BF16)
        ds_ref[prompt:, at] = dscore[shard:].astype(BF16)

    grad_latent = dot(ds_ref[...], q_ref[...], NN) + dot(p_scr[...], up_ref[...], NN)
    grad_rope = dot(ds_ref[...], qr_ref[...], NN)

    piece = tok // n_seq
    own_rope = grad_rope[prompt:]
    own_rope = own_rope + pltpu.roll(own_rope, rope, 1)
    for s in range(n_seq):
        parts = [
            grad_latent[prompt + s * piece : prompt + (s + 1) * piece, c : c + 2 * rope]
            for c in range(0, latent, 2 * rope)
        ]
        parts.append(own_rope[s * piece : (s + 1) * piece])
        span_out[s ^ my_seq] = jnp.concatenate(parts, axis=0).astype(BF16)

    cols = full // n_resp
    my_pair = my_resp // 2
    scale_twice = jnp.concatenate([scale[:, latent:]] * 2, axis=1)
    pairs = n_seq // 2 - 1
    for slot in range(n_seq):
        at = slice(slot * shard, (slot + 1) * shard)
        lat = (grad_latent[at] * scale[:, :latent]).T
        rot = (grad_rope[at] * scale_twice).T
        whole = jnp.concatenate([lat, rot[:rope] + rot[rope:]], axis=0)
        for z in range(n_resp // 2):
            even_part = whole[2 * z * cols : (2 * z + 1) * cols]
            odd_part = whole[(2 * z + 1) * cols : (2 * z + 2) * cols]
            mine = jnp.where(odd, odd_part, even_part).astype(BF16)
            theirs = jnp.where(odd, even_part, odd_part).astype(BF16)
            if slot in (0, n_seq - 1):
                d = slot
            elif slot <= pairs:
                d = 2 * slot - 1 + my_resp % 2
            else:
                d = 2 * (slot - pairs) - my_resp % 2
            mine_ref[d, z ^ my_pair] = mine
            theirs_ref[d, z ^ my_pair] = theirs


def sum_kernel(mine_ref, theirs_ref, span_ref, own_ref, *pay_refs):
    pairs, cols, lanes = mine_ref.shape[1:]
    for d in range(len(pay_refs) + 1):
        for z in range(pairs):
            total = mine_ref[d, z].astype(F32) + theirs_ref[d, z].astype(F32)
            if d == 0:
                own_ref[z] = total
            else:
                pay_refs[d - 1][pl.ds(z * cols, cols), :] = total.astype(BF16)
        if d:
            pay_refs[d - 1][pl.ds(pairs * cols, span_ref.shape[1]), :] = span_ref[d]


def query_kernel(heads, first, count, ds_ref, keys_ref, *refs):
    out_hbm, rope_hbm, out_v, rope_v, rope_scr, out_sems, rope_sems = refs[-7:]
    latent = out_v.shape[1]
    rope = (keys_ref.shape[1] - latent) // 2
    step = 16 * heads
    low = low_half((16, 2 * rope), rope)
    copies = []
    for i in range(count):
        at = pl.ds((first + i) * step, step)
        here = pl.ds(i * step, step)
        out_v[here, :] = dot(ds_ref[:, at], keys_ref[:, :latent], TN).astype(BF16)
        copies.append(pltpu.make_async_copy(out_v.at[here], out_hbm.at[at], out_sems.at[i]))
        copies[-1].start()
        rope_scr[...] = dot(ds_ref[:, at], keys_ref[:, latent:], TN)
        for j in range(heads // 2):
            even = rope_scr[pl.ds(2 * j, 16, stride=heads), :]
            odd = rope_scr[pl.ds(2 * j + 1, 16, stride=heads), :]
            rope_v[pl.ds(i * 16, 16), pl.ds(2 * rope * j, 2 * rope)] = jnp.where(
                low, even, odd
            ).astype(BF16)
        copies.append(
            pltpu.make_async_copy(
                rope_v.at[pl.ds(i * 16, 16)],
                rope_hbm.at[pl.ds((first + i) * 16, 16)],
                rope_sems.at[i],
            )
        )
        copies[-1].start()
    for copy in copies:
        copy.wait()


def on_device(
    n_resp,
    n_seq,
    prompt_cache,
    channel_scale,
    span_cache,
    q_latent,
    q_rope,
    d_out,
    resp_length,
    span_response,
    span_index,
):
    tok, heads, latent = q_latent.shape
    shard, full = prompt_cache.shape
    rope = full - latent
    rows = tok * heads
    prompt = shard * n_seq
    keys = prompt + tok
    early = shard + tok
    width = latent + 2 * rope
    cols = full // n_resp
    pairs = n_resp // 2
    piece = tok // n_seq
    span_rows = piece * (latent // (2 * rope) + 1)
    vmem = pl.BlockSpec(memory_space=pltpu.VMEM)
    hbm = pl.BlockSpec(memory_space=pl.ANY)

    def shape(dims, dtype=BF16):
        return jax.ShapeDtypeStruct(dims, dtype)

    def over_seq(x, d):
        return lax.ppermute(x, "seq", [(i, i ^ d) for i in range(n_seq)])

    def over_resp(x, d):
        return lax.ppermute(x, "resp", [(i, i ^ d) for i in range(n_resp)])

    def by_core(x, d):
        moves = [
            (r * n_seq + s, r * n_seq + (s ^ (d + r % 2)))
            for r in range(n_resp)
            for s in range(n_seq)
        ]
        return lax.ppermute(x, ("resp", "seq"), moves)

    prompt_t = prompt_cache.T
    fetched = [by_core(prompt_t, d) for d in range(1, n_seq - 1, 2)]

    scale_row = channel_scale.reshape(1, full)
    smem = pl.BlockSpec(memory_space=pltpu.SMEM)
    q_rows = q_latent.reshape(rows, latent)
    up_rows = d_out.reshape(rows, latent)
    mask = pl.pallas_call(
        functools.partial(mask_kernel, heads),
        out_shape=shape((tok, rows), F32),
        out_specs=vmem,
        compiler_params=pltpu.CompilerParams(vmem_limit_bytes=4 * MIB),
        cost_estimate=pl.CostEstimate(
            flops=40 * keys * rows * width, bytes_accessed=4 * tok * rows, transcendentals=0
        ),
        name="mask",
    )()
    again, mask = lax.optimization_barrier((prompt_t, mask))
    last = over_seq(again, n_seq - 1)
    q_turned, expo, dprob, stats, early_keys = pl.pallas_call(
        functools.partial(early_kernel, heads),
        out_shape=(
            shape((rows, 2 * rope)),
            shape((early, rows), F32),
            shape((early, rows), F32),
            shape((8, rows), F32),
            shape((early, width)),
        ),
        in_specs=[smem] * 3 + [vmem] * 7,
        out_specs=(vmem,) * 5,
        scratch_shapes=[pltpu.VMEM((rows, 2 * rope), F32)],
        compiler_params=pltpu.CompilerParams(vmem_limit_bytes=24 * MIB),
        cost_estimate=pl.CostEstimate(
            flops=2 * early * rows * 2 * latent, bytes_accessed=4 * rows * latent, transcendentals=0
        ),
        name="early",
    )(
        resp_length,
        span_response,
        span_index,
        mask,
        scale_row,
        prompt_t,
        span_cache,
        q_rows,
        q_rope,
        up_rows,
    )

    fetched, stats = lax.optimization_barrier((fetched, stats))
    swapped = [over_resp(value, 1) for value in fetched]
    middle = shard * len(fetched)
    expo_b, dprob_b, stats, middle_keys = pl.pallas_call(
        middle_kernel,
        out_shape=(
            shape((middle, rows), F32),
            shape((middle, rows), F32),
            shape((8, rows), F32),
            shape((middle, width)),
        ),
        in_specs=[vmem] * (5 + len(fetched)),
        out_specs=(vmem,) * 4,
        compiler_params=pltpu.CompilerParams(vmem_limit_bytes=24 * MIB),
        cost_estimate=pl.CostEstimate(
            flops=2 * middle * rows * 2 * latent, bytes_accessed=4 * rows * latent, transcendentals=0
        ),
        name="middle",
    )(scale_row, q_rows, up_rows, q_turned, stats, *fetched)

    mine, theirs, span, dscore, keys_all = pl.pallas_call(
        functools.partial(keys_kernel, n_resp, n_seq),
        out_shape=(
            shape((n_seq, pairs, cols, shard)),
            shape((n_seq, pairs, cols, shard)),
            shape((n_seq, span_rows, 2 * rope)),
            shape((keys, rows)),
            shape((keys, width)),
        ),
        in_specs=[vmem] * (12 + len(swapped)),
        out_specs=(vmem,) * 5,
        scratch_shapes=[
            pltpu.VMEM((keys, rows), BF16),
            pltpu.VMEM((shard * (len(swapped) + 1), width), BF16),
        ],
        compiler_params=pltpu.CompilerParams(vmem_limit_bytes=24 * MIB),
        cost_estimate=pl.CostEstimate(
            flops=2 * keys * rows * 3 * latent, bytes_accessed=4 * rows * latent, transcendentals=0
        ),
        name="keys",
    )(
        scale_row,
        q_rows,
        up_rows,
        q_turned,
        expo,
        dprob,
        early_keys,
        expo_b,
        dprob_b,
        middle_keys,
        stats,
        *swapped,
        last,
    )

    steps = tok // 16

    def queries(first, count, dscore, keys_all, before):
        return pl.pallas_call(
            functools.partial(query_kernel, heads, first, count),
            out_shape=(shape((rows, latent)), shape((tok, heads * rope))),
            in_specs=[vmem] * 2 + [hbm] * len(before),
            out_specs=(hbm,) * 2,
            scratch_shapes=[
                pltpu.VMEM((count * 16 * heads, latent), BF16),
                pltpu.VMEM((count * 16, heads * rope), BF16),
                pltpu.VMEM((16 * heads, 2 * rope), F32),
                pltpu.SemaphoreType.DMA((count,)),
                pltpu.SemaphoreType.DMA((count,)),
            ],
            input_output_aliases={2: 0, 3: 1} if before else {},
            compiler_params=pltpu.CompilerParams(vmem_limit_bytes=16 * MIB),
            cost_estimate=pl.CostEstimate(
                flops=2 * keys * count * 16 * heads * width,
                bytes_accessed=count * 32 * heads * latent,
                transcendentals=0,
            ),
            name="queries",
        )(dscore, keys_all, *before)

    theirs = over_resp(theirs, 1)
    farthest = mine[-1].astype(F32) + theirs[-1].astype(F32)
    farthest = jnp.concatenate(
        [farthest.astype(BF16).reshape(-1, 2 * rope), span[-1]], axis=0
    )
    moved = [over_seq(farthest, n_seq - 1)]
    block, *pays = pl.pallas_call(
        sum_kernel,
        out_shape=[shape((pairs, cols, shard), F32)]
        + [shape((pairs * cols + span_rows, shard))] * (n_seq - 2),
        in_specs=[vmem] * 3,
        out_specs=[vmem] * (n_seq - 1),
        compiler_params=pltpu.CompilerParams(vmem_limit_bytes=8 * MIB),
        cost_estimate=pl.CostEstimate(
            flops=keys * rows * width, bytes_accessed=4 * keys * width, transcendentals=0
        ),
        name="sums",
    )(mine, theirs, span)
    moved += [over_seq(pay, d + 1) for d, pay in enumerate(pays)]
    half = (3 * steps + 3) // 4
    partly = queries(0, half, dscore, keys_all, ())
    split = pairs * cols
    own = span[0].astype(F32)
    for x in moved:
        block = block + x[:split].reshape(pairs, cols, shard).astype(F32)
        own = own + x[split:].astype(F32)
    block_half = block.astype(BF16)
    block_half, dscore, keys_all = lax.optimization_barrier((block_half, dscore, keys_all))
    arrived = [over_resp(block_half[d], 2 * d) for d in range(pairs - 1, 0, -1)]
    grad_latent, grad_rope = queries(half, steps - half, dscore, keys_all, partly)
    total = block[0]
    for x in arrived:
        total = total + x.astype(F32)
    grad_prompt = total.T

    parts = own.reshape(-1, piece, 2 * rope)
    grad_span = jnp.concatenate(
        [parts[i] for i in range(latent // (2 * rope))] + [parts[-1][:, :rope]], axis=1
    )
    return (
        grad_latent.reshape(tok, heads, latent),
        grad_rope,
        grad_prompt,
        grad_span,
    )


def solution(mesh):
    return jax.shard_map(
        functools.partial(on_device, mesh.shape["resp"], mesh.shape["seq"]),
        mesh=mesh,
        in_specs=(
            P("seq", None),
            P(),
            P("resp", None),
            P("resp", "seq", None),
            P("resp", "seq"),
            P("resp", "seq", None),
            P(),
            P(),
            P(),
        ),
        out_specs=(
            P("resp", "seq", None),
            P("resp", "seq"),
            P("seq", "resp"),
            P(("resp", "seq"), None),
        ),
        check_vma=False,
    )
```

```python
import functools
import math

import jax
import jax.numpy as jnp
from jax import lax
from jax.experimental import pallas as pl
from jax.experimental.pallas import tpu as pltpu
from jax.sharding import PartitionSpec as P

SIGMA = 1.0 / math.sqrt(192.0)
EXP_SCALE = SIGMA * math.log2(math.e)
F32 = jnp.float32
BF16 = jnp.bfloat16
NT = (((1,), (1,)), ((), ()))
NN = (((1,), (0,)), ((), ()))
TN = (((0,), (0,)), ((), ()))
MIB = 1024 * 1024
STEP = 256


def dot(a, b, dims):
    return lax.dot_general(a, b, dims, preferred_element_type=F32)


def low_half(shape, half):
    return lax.broadcasted_iota(jnp.int32, shape, len(shape) - 1) < half


def put_keys(keys_ref, start, latent, values):
    rows, full = values.shape
    keys_ref[pl.ds(start, rows), :full] = values
    keys_ref[pl.ds(start, rows), full:] = values[:, latent:]


def scaled_rows(shard, scale):
    return (shard.astype(F32).T * scale).astype(BF16)


def mask_kernel(heads, mask_ref):
    key_pos = lax.broadcasted_iota(jnp.int32, mask_ref.shape, 0)
    row = lax.broadcasted_iota(jnp.int32, mask_ref.shape, 1)
    mask_ref[...] = jnp.where(key_pos * heads <= row, 1.0, 0.0)


def partial_softmax(keys_ref, at, q_ref, qr_ref, up_ref):
    latent = q_ref.shape[1]
    logits = dot(keys_ref[:, :latent], q_ref[at, :], NT) + dot(
        keys_ref[:, latent:], qr_ref[at, :], NT
    )
    return logits, dot(keys_ref[:, :latent], up_ref[at, :], NT) * SIGMA


def early_kernel(
    heads,
    length_s,
    response_s,
    index_s,
    mask_ref,
    scale_ref,
    prompt_ref,
    span_ref,
    q_ref,
    qrope_v,
    up_ref,
    qr_ref,
    expo_ref,
    dprob_ref,
    stat_ref,
    keys_ref,
    rope_scr,
):
    full, shard = prompt_ref.shape
    tok = span_ref.shape[0]
    rows, latent = q_ref.shape
    rope = full - latent
    my_resp = lax.axis_index("resp")
    live = jnp.clip(
        length_s[response_s[my_resp]] - index_s[my_resp] * tok, 0, tok
    )
    low = low_half((tok, 2 * rope), rope)
    for j in range(heads // 2):
        x = qrope_v[:, pl.ds(2 * rope * j, 2 * rope)].astype(F32)
        rope_scr[pl.ds(2 * j, tok, stride=heads), :] = jnp.where(low, x, 0.0)
        rope_scr[pl.ds(2 * j + 1, tok, stride=heads), :] = jnp.where(low, 0.0, x)
    qr_ref[...] = rope_scr[...].astype(BF16)

    put_keys(keys_ref, 0, latent, scaled_rows(prompt_ref[...], scale_ref[...]))
    put_keys(keys_ref, shard, latent, span_ref[...])

    for i in range(rows // STEP):
        at = pl.ds(i * STEP, STEP)
        logits, dprob = partial_softmax(keys_ref, at, q_ref, qr_ref, up_ref)
        key_pos = lax.broadcasted_iota(jnp.int32, (tok, STEP), 0)
        seen = (mask_ref[:, at] > 0.5) & (key_pos < live)
        own = jnp.where(seen, logits[shard:], -jnp.inf)
        logits = jnp.concatenate([logits[:shard], own], axis=0)
        top = jnp.max(logits, axis=0, keepdims=True)
        expo = jnp.exp2((logits - top) * EXP_SCALE)
        row_pos = (lax.broadcasted_iota(jnp.int32, (1, STEP), 1) + i * STEP) // heads
        expo_ref[:, at] = expo
        dprob_ref[:, at] = dprob
        stat_ref[0:1, at] = top
        stat_ref[1:2, at] = jnp.sum(expo, axis=0, keepdims=True)
        stat_ref[2:3, at] = jnp.sum(expo * dprob, axis=0, keepdims=True)
        stat_ref[3:4, at] = jnp.where(row_pos < live, 1.0, 0.0)


def middle_kernel(scale_ref, q_ref, up_ref, qr_ref, stat_ref, *refs):
    shard_refs = refs[:-4]
    expo_ref, dprob_ref, out_ref, keys_ref = refs[-4:]
    rows, latent = q_ref.shape
    shard = shard_refs[0].shape[1]
    for d, ref in enumerate(shard_refs):
        put_keys(keys_ref, d * shard, latent, scaled_rows(ref[...], scale_ref[...]))
    for i in range(rows // STEP):
        at = pl.ds(i * STEP, STEP)
        logits, dprob = partial_softmax(keys_ref, at, q_ref, qr_ref, up_ref)
        before = stat_ref[0:1, at]
        top = jnp.maximum(before, jnp.max(logits, axis=0, keepdims=True))
        expo = jnp.exp2((logits - top) * EXP_SCALE)
        again = jnp.exp2((before - top) * EXP_SCALE)
        expo_ref[:, at] = expo
        dprob_ref[:, at] = dprob
        out_ref[0:1, at] = top
        out_ref[1:2, at] = stat_ref[1:2, at] * again + jnp.sum(expo, axis=0, keepdims=True)
        out_ref[2:3, at] = stat_ref[2:3, at] * again + jnp.sum(
            expo * dprob, axis=0, keepdims=True
        )
        out_ref[3:4, at] = stat_ref[3:4, at]
        out_ref[4:5, at] = before


def keys_kernel(
    n_resp,
    n_seq,
    scale_ref,
    q_ref,
    up_ref,
    qr_ref,
    expo_a,
    dprob_a,
    keys_a,
    expo_b,
    dprob_b,
    keys_b,
    stat_ref,
    *refs,
):
    shard_refs = refs[:-8]
    mine_ref, theirs_ref, far_ref, span_out, ds_ref, keys_ref, p_scr, keys_c = refs[-8:]
    rows, latent = q_ref.shape
    full = scale_ref.shape[1]
    shard = shard_refs[0].shape[1]
    rope = full - latent
    prompt = shard * n_seq
    tok = keys_a.shape[0] - shard
    my_resp = lax.axis_index("resp")
    my_seq = lax.axis_index("seq")
    odd = (my_resp % 2) == 1

    middle = slice(shard, shard + keys_b.shape[0])
    late = slice(middle.stop, prompt)
    scale = scale_ref[...]
    for d, ref in enumerate(shard_refs):
        put_keys(keys_c, d * shard, latent, scaled_rows(ref[...], scale))
    keys_ref[:shard] = keys_a[:shard]
    keys_ref[middle] = keys_b[...]
    keys_ref[late] = keys_c[...]
    keys_ref[prompt:] = keys_a[shard:]

    for i in range(rows // STEP):
        at = pl.ds(i * STEP, STEP)
        logits, dprob = partial_softmax(keys_c, at, q_ref, qr_ref, up_ref)
        before = stat_ref[0:1, at]
        top = jnp.maximum(before, jnp.max(logits, axis=0, keepdims=True))
        expo = jnp.exp2((logits - top) * EXP_SCALE)
        again = jnp.exp2((before - top) * EXP_SCALE)
        total = stat_ref[1:2, at] * again + jnp.sum(expo, axis=0, keepdims=True)
        weighed = stat_ref[2:3, at] * again + jnp.sum(expo * dprob, axis=0, keepdims=True)
        inverse = 1.0 / total
        delta = weighed * inverse
        factor = inverse * stat_ref[3:4, at]
        probs = expo * factor
        p_scr[late, at] = probs.astype(BF16)
        ds_ref[late, at] = (probs * (dprob - delta)).astype(BF16)
        probs = expo_b[:, at] * (factor * again)
        p_scr[middle, at] = probs.astype(BF16)
        ds_ref[middle, at] = (probs * (dprob_b[:, at] - delta)).astype(BF16)
        first = jnp.exp2((stat_ref[4:5, at] - top) * EXP_SCALE)
        probs = expo_a[:, at] * (factor * first)
        dscore = probs * (dprob_a[:, at] - delta)
        p_scr[:shard, at] = probs[:shard].astype(BF16)
        ds_ref[:shard, at] = dscore[:shard].astype(BF16)
        p_scr[prompt:, at] = probs[shard:].astype(BF16)
        ds_ref[prompt:, at] = dscore[shard:].astype(BF16)

    grad_latent = dot(ds_ref[...], q_ref[...], NN) + dot(p_scr[...], up_ref[...], NN)
    grad_rope = dot(ds_ref[...], qr_ref[...], NN)

    piece = tok // n_seq
    own_rope = grad_rope[prompt:]
    own_rope = own_rope + pltpu.roll(own_rope, rope, 1)
    for s in range(n_seq):
        parts = [
            grad_latent[prompt + s * piece : prompt + (s + 1) * piece, c : c + 2 * rope]
            for c in range(0, latent, 2 * rope)
        ]
        parts.append(own_rope[s * piece : (s + 1) * piece])
        span_out[s ^ my_seq] = jnp.concatenate(parts, axis=0).astype(BF16)

    cols = full // n_resp
    my_pair = my_resp // 2
    scale_twice = jnp.concatenate([scale[:, latent:]] * 2, axis=1)
    pairs = n_seq // 2 - 1
    for slot in range(n_seq):
        at = slice(slot * shard, (slot + 1) * shard)
        lat = (grad_latent[at] * scale[:, :latent]).T
        rot = (grad_rope[at] * scale_twice).T
        whole = jnp.concatenate([lat, rot[:rope] + rot[rope:]], axis=0)
        for z in range(n_resp // 2):
            even_part = whole[2 * z * cols : (2 * z + 1) * cols]
            odd_part = whole[(2 * z + 1) * cols : (2 * z + 2) * cols]
            mine = jnp.where(odd, odd_part, even_part).astype(BF16)
            theirs = jnp.where(odd, even_part, odd_part).astype(BF16)
            if slot in (0, n_seq - 1):
                d = slot
            elif slot <= pairs:
                d = 2 * slot - 1 + my_resp % 2
            else:
                d = 2 * (slot - pairs) - my_resp % 2
            mine_ref[d, z ^ my_pair] = mine
            if slot == n_seq - 1:
                far_ref[z ^ my_pair] = theirs
            else:
                theirs_ref[d, z ^ my_pair] = theirs


def sum_kernel(mine_ref, theirs_ref, span_ref, own_ref, *pay_refs):
    pairs, cols, lanes = mine_ref.shape[1:]
    for d in range(len(pay_refs) + 1):
        for z in range(pairs):
            total = mine_ref[d, z].astype(F32) + theirs_ref[d, z].astype(F32)
            if d == 0:
                own_ref[z] = total
            else:
                pay_refs[d - 1][pl.ds(z * cols, cols), :] = total.astype(BF16)
        if d:
            pay_refs[d - 1][pl.ds(pairs * cols, span_ref.shape[1]), :] = span_ref[d]


def query_kernel(
    heads, ds_ref, keys_ref, out_hbm, rope_hbm, out_v, rope_v, rope_scr, out_sems, rope_sems
):
    latent = out_v.shape[1]
    rope = (keys_ref.shape[1] - latent) // 2
    step = 16 * heads
    low = low_half((16, 2 * rope), rope)
    copies = []
    for i in range(out_v.shape[0] // step):
        at = pl.ds(i * step, step)
        out_v[at, :] = dot(ds_ref[:, at], keys_ref[:, :latent], TN).astype(BF16)
        copies.append(pltpu.make_async_copy(out_v.at[at], out_hbm.at[at], out_sems.at[i]))
        copies[-1].start()
        rope_scr[...] = dot(ds_ref[:, at], keys_ref[:, latent:], TN)
        for j in range(heads // 2):
            even = rope_scr[pl.ds(2 * j, 16, stride=heads), :]
            odd = rope_scr[pl.ds(2 * j + 1, 16, stride=heads), :]
            rope_v[pl.ds(i * 16, 16), pl.ds(2 * rope * j, 2 * rope)] = jnp.where(
                low, even, odd
            ).astype(BF16)
        copies.append(
            pltpu.make_async_copy(
                rope_v.at[pl.ds(i * 16, 16)],
                rope_hbm.at[pl.ds(i * 16, 16)],
                rope_sems.at[i],
            )
        )
        copies[-1].start()
    for copy in copies:
        copy.wait()


def on_device(
    n_resp,
    n_seq,
    prompt_cache,
    channel_scale,
    span_cache,
    q_latent,
    q_rope,
    d_out,
    resp_length,
    span_response,
    span_index,
):
    tok, heads, latent = q_latent.shape
    shard, full = prompt_cache.shape
    rope = full - latent
    rows = tok * heads
    prompt = shard * n_seq
    keys = prompt + tok
    early = shard + tok
    width = latent + 2 * rope
    cols = full // n_resp
    pairs = n_resp // 2
    piece = tok // n_seq
    span_rows = piece * (latent // (2 * rope) + 1)
    vmem = pl.BlockSpec(memory_space=pltpu.VMEM)
    hbm = pl.BlockSpec(memory_space=pl.ANY)

    def shape(dims, dtype=BF16):
        return jax.ShapeDtypeStruct(dims, dtype)

    def over_seq(x, d):
        return lax.ppermute(x, "seq", [(i, i ^ d) for i in range(n_seq)])

    def over_resp(x, d):
        return lax.ppermute(x, "resp", [(i, i ^ d) for i in range(n_resp)])

    def by_core(x, d):
        moves = [
            (r * n_seq + s, r * n_seq + (s ^ (d + r % 2)))
            for r in range(n_resp)
            for s in range(n_seq)
        ]
        return lax.ppermute(x, ("resp", "seq"), moves)

    prompt_t = prompt_cache.T
    fetched = [by_core(prompt_t, d) for d in range(1, n_seq - 1, 2)]

    scale_row = channel_scale.reshape(1, full)
    smem = pl.BlockSpec(memory_space=pltpu.SMEM)
    q_rows = q_latent.reshape(rows, latent)
    up_rows = d_out.reshape(rows, latent)
    mask = pl.pallas_call(
        functools.partial(mask_kernel, heads),
        out_shape=shape((tok, rows), F32),
        out_specs=vmem,
        compiler_params=pltpu.CompilerParams(vmem_limit_bytes=4 * MIB),
        cost_estimate=pl.CostEstimate(
            flops=40 * keys * rows * width, bytes_accessed=4 * tok * rows, transcendentals=0
        ),
        name="mask",
    )()
    again, mask = lax.optimization_barrier((prompt_t, mask))
    last = over_seq(again, n_seq - 1)
    q_turned, expo, dprob, stats, early_keys = pl.pallas_call(
        functools.partial(early_kernel, heads),
        out_shape=(
            shape((rows, 2 * rope)),
            shape((early, rows), F32),
            shape((early, rows), F32),
            shape((8, rows), F32),
            shape((early, width)),
        ),
        in_specs=[smem] * 3 + [vmem] * 7,
        out_specs=(vmem,) * 5,
        scratch_shapes=[pltpu.VMEM((rows, 2 * rope), F32)],
        compiler_params=pltpu.CompilerParams(vmem_limit_bytes=24 * MIB),
        cost_estimate=pl.CostEstimate(
            flops=2 * early * rows * 2 * latent, bytes_accessed=4 * rows * latent, transcendentals=0
        ),
        name="early",
    )(
        resp_length,
        span_response,
        span_index,
        mask,
        scale_row,
        prompt_t,
        span_cache,
        q_rows,
        q_rope,
        up_rows,
    )

    fetched, stats = lax.optimization_barrier((fetched, stats))
    swapped = [over_resp(value, 1) for value in fetched]
    middle = shard * len(fetched)
    expo_b, dprob_b, stats, middle_keys = pl.pallas_call(
        middle_kernel,
        out_shape=(
            shape((middle, rows), F32),
            shape((middle, rows), F32),
            shape((8, rows), F32),
            shape((middle, width)),
        ),
        in_specs=[vmem] * (5 + len(fetched)),
        out_specs=(vmem,) * 4,
        compiler_params=pltpu.CompilerParams(vmem_limit_bytes=24 * MIB),
        cost_estimate=pl.CostEstimate(
            flops=2 * middle * rows * 2 * latent, bytes_accessed=4 * rows * latent, transcendentals=0
        ),
        name="middle",
    )(scale_row, q_rows, up_rows, q_turned, stats, *fetched)

    mine, theirs, far, span, dscore, keys_all = pl.pallas_call(
        functools.partial(keys_kernel, n_resp, n_seq),
        out_shape=(
            shape((n_seq, pairs, cols, shard)),
            shape((n_seq - 1, pairs, cols, shard)),
            shape((pairs, cols, shard)),
            shape((n_seq, span_rows, 2 * rope)),
            shape((keys, rows)),
            shape((keys, width)),
        ),
        in_specs=[vmem] * (12 + len(swapped)),
        out_specs=(vmem,) * 6,
        scratch_shapes=[
            pltpu.VMEM((keys, rows), BF16),
            pltpu.VMEM((shard * (len(swapped) + 1), width), BF16),
        ],
        compiler_params=pltpu.CompilerParams(vmem_limit_bytes=24 * MIB),
        cost_estimate=pl.CostEstimate(
            flops=2 * keys * rows * 3 * latent, bytes_accessed=4 * rows * latent, transcendentals=0
        ),
        name="keys",
    )(
        scale_row,
        q_rows,
        up_rows,
        q_turned,
        expo,
        dprob,
        early_keys,
        expo_b,
        dprob_b,
        middle_keys,
        stats,
        *swapped,
        last,
    )

    steps = tok // 16

    def queries(dscore, keys_all):
        return pl.pallas_call(
            functools.partial(query_kernel, heads),
            out_shape=(shape((rows, latent)), shape((tok, heads * rope))),
            in_specs=[vmem] * 2,
            out_specs=(hbm,) * 2,
            scratch_shapes=[
                pltpu.VMEM((rows, latent), BF16),
                pltpu.VMEM((tok, heads * rope), BF16),
                pltpu.VMEM((16 * heads, 2 * rope), F32),
                pltpu.SemaphoreType.DMA((steps,)),
                pltpu.SemaphoreType.DMA((steps,)),
            ],
            compiler_params=pltpu.CompilerParams(vmem_limit_bytes=16 * MIB),
            cost_estimate=pl.CostEstimate(
                flops=2 * keys * rows * width, bytes_accessed=2 * rows * width, transcendentals=0
            ),
            name="queries",
        )(dscore, keys_all)

    far = over_resp(far, 1)
    theirs = over_resp(theirs, 1)
    farthest = mine[-1].astype(F32) + far.astype(F32)
    farthest = jnp.concatenate(
        [farthest.astype(BF16).reshape(-1, 2 * rope), span[-1]], axis=0
    )
    moved = [over_seq(farthest, n_seq - 1)]
    block, *pays = pl.pallas_call(
        sum_kernel,
        out_shape=[shape((pairs, cols, shard), F32)]
        + [shape((pairs * cols + span_rows, shard))] * (n_seq - 2),
        in_specs=[vmem] * 3,
        out_specs=[vmem] * (n_seq - 1),
        compiler_params=pltpu.CompilerParams(vmem_limit_bytes=8 * MIB),
        cost_estimate=pl.CostEstimate(
            flops=keys * rows * width, bytes_accessed=4 * keys * width, transcendentals=0
        ),
        name="sums",
    )(mine, theirs, span)
    moved += [over_seq(pay, d + 1) for d, pay in enumerate(pays)]
    grad_latent, grad_rope = queries(dscore, keys_all)
    split = pairs * cols
    own = span[0].astype(F32)
    for x in moved:
        block = block + x[:split].reshape(pairs, cols, shard).astype(F32)
        own = own + x[split:].astype(F32)
    block_half = block.astype(BF16)
    arrived = [over_resp(block_half[d], 2 * d) for d in range(pairs - 1, 0, -1)]
    total = block[0]
    for x in arrived:
        total = total + x.astype(F32)
    grad_prompt = total.T

    parts = own.reshape(-1, piece, 2 * rope)
    grad_span = jnp.concatenate(
        [parts[i] for i in range(latent // (2 * rope))] + [parts[-1][:, :rope]], axis=1
    )
    return (
        grad_latent.reshape(tok, heads, latent),
        grad_rope,
        grad_prompt,
        grad_span,
    )


def solution(mesh):
    return jax.shard_map(
        functools.partial(on_device, mesh.shape["resp"], mesh.shape["seq"]),
        mesh=mesh,
        in_specs=(
            P("seq", None),
            P(),
            P("resp", None),
            P("resp", "seq", None),
            P("resp", "seq"),
            P("resp", "seq", None),
            P(),
            P(),
            P(),
        ),
        out_specs=(
            P("resp", "seq", None),
            P("resp", "seq"),
            P("seq", "resp"),
            P(("resp", "seq"), None),
        ),
        check_vma=False,
    )
```

```python
import functools
import math

import jax
import jax.numpy as jnp
from jax import lax
from jax.experimental import pallas as pl
from jax.experimental.pallas import tpu as pltpu
from jax.sharding import PartitionSpec as P

SIGMA = 1.0 / math.sqrt(192.0)
EXP_SCALE = SIGMA * math.log2(math.e)
F32 = jnp.float32
BF16 = jnp.bfloat16
NT = (((1,), (1,)), ((), ()))
NN = (((1,), (0,)), ((), ()))
TN = (((0,), (0,)), ((), ()))
MIB = 1024 * 1024
STEP = 256


def dot(a, b, dims):
    return lax.dot_general(a, b, dims, preferred_element_type=F32)


def low_half(shape, half):
    return lax.broadcasted_iota(jnp.int32, shape, len(shape) - 1) < half


def put_keys(keys_ref, start, latent, values):
    rows, full = values.shape
    keys_ref[pl.ds(start, rows), :full] = values
    keys_ref[pl.ds(start, rows), full:] = values[:, latent:]


def scaled_rows(shard, scale):
    return (shard.astype(F32).T * scale).astype(BF16)


def mask_kernel(heads, mask_ref):
    key_pos = lax.broadcasted_iota(jnp.int32, mask_ref.shape, 0)
    row = lax.broadcasted_iota(jnp.int32, mask_ref.shape, 1)
    mask_ref[...] = jnp.where(key_pos * heads <= row, 1.0, 0.0)


def partial_softmax(keys_ref, at, q_ref, qr_ref, up_ref):
    latent = q_ref.shape[1]
    logits = dot(keys_ref[:, :latent], q_ref[at, :], NT) + dot(
        keys_ref[:, latent:], qr_ref[at, :], NT
    )
    return logits, dot(keys_ref[:, :latent], up_ref[at, :], NT) * SIGMA


def early_kernel(
    heads,
    length_s,
    response_s,
    index_s,
    mask_ref,
    scale_ref,
    prompt_ref,
    span_ref,
    q_ref,
    qrope_v,
    up_ref,
    qr_ref,
    expo_ref,
    dprob_ref,
    stat_ref,
    keys_ref,
    rope_scr,
):
    full, shard = prompt_ref.shape
    tok = span_ref.shape[0]
    rows, latent = q_ref.shape
    rope = full - latent
    my_resp = lax.axis_index("resp")
    live = jnp.clip(
        length_s[response_s[my_resp]] - index_s[my_resp] * tok, 0, tok
    )
    low = low_half((tok, 2 * rope), rope)
    for j in range(heads // 2):
        x = qrope_v[:, pl.ds(2 * rope * j, 2 * rope)].astype(F32)
        rope_scr[pl.ds(2 * j, tok, stride=heads), :] = jnp.where(low, x, 0.0)
        rope_scr[pl.ds(2 * j + 1, tok, stride=heads), :] = jnp.where(low, 0.0, x)
    qr_ref[...] = rope_scr[...].astype(BF16)

    put_keys(keys_ref, 0, latent, scaled_rows(prompt_ref[...], scale_ref[...]))
    put_keys(keys_ref, shard, latent, span_ref[...])

    for i in range(rows // STEP):
        at = pl.ds(i * STEP, STEP)
        logits, dprob = partial_softmax(keys_ref, at, q_ref, qr_ref, up_ref)
        key_pos = lax.broadcasted_iota(jnp.int32, (tok, STEP), 0)
        seen = (mask_ref[:, at] > 0.5) & (key_pos < live)
        own = jnp.where(seen, logits[shard:], -jnp.inf)
        logits = jnp.concatenate([logits[:shard], own], axis=0)
        top = jnp.max(logits, axis=0, keepdims=True)
        expo = jnp.exp2((logits - top) * EXP_SCALE)
        row_pos = (lax.broadcasted_iota(jnp.int32, (1, STEP), 1) + i * STEP) // heads
        expo_ref[:, at] = expo
        dprob_ref[:, at] = dprob
        stat_ref[0:1, at] = top
        stat_ref[1:2, at] = jnp.sum(expo, axis=0, keepdims=True)
        stat_ref[2:3, at] = jnp.sum(expo * dprob, axis=0, keepdims=True)
        stat_ref[3:4, at] = jnp.where(row_pos < live, 1.0, 0.0)


def middle_kernel(scale_ref, q_ref, up_ref, qr_ref, stat_ref, *refs):
    shard_refs = refs[:-4]
    expo_ref, dprob_ref, out_ref, keys_ref = refs[-4:]
    rows, latent = q_ref.shape
    shard = shard_refs[0].shape[1]
    for d, ref in enumerate(shard_refs):
        put_keys(keys_ref, d * shard, latent, scaled_rows(ref[...], scale_ref[...]))
    for i in range(rows // STEP):
        at = pl.ds(i * STEP, STEP)
        logits, dprob = partial_softmax(keys_ref, at, q_ref, qr_ref, up_ref)
        before = stat_ref[0:1, at]
        top = jnp.maximum(before, jnp.max(logits, axis=0, keepdims=True))
        expo = jnp.exp2((logits - top) * EXP_SCALE)
        again = jnp.exp2((before - top) * EXP_SCALE)
        expo_ref[:, at] = expo
        dprob_ref[:, at] = dprob
        out_ref[0:1, at] = top
        out_ref[1:2, at] = stat_ref[1:2, at] * again + jnp.sum(expo, axis=0, keepdims=True)
        out_ref[2:3, at] = stat_ref[2:3, at] * again + jnp.sum(
            expo * dprob, axis=0, keepdims=True
        )
        out_ref[3:4, at] = stat_ref[3:4, at]
        out_ref[4:5, at] = before


def keys_kernel(
    n_resp,
    n_seq,
    scale_ref,
    q_ref,
    up_ref,
    qr_ref,
    expo_a,
    dprob_a,
    keys_a,
    expo_b,
    dprob_b,
    keys_b,
    stat_ref,
    *refs,
):
    shard_refs = refs[:-8]
    mine_ref, theirs_ref, far_ref, span_out, ds_ref, keys_ref, p_scr, keys_c = refs[-8:]
    rows, latent = q_ref.shape
    full = scale_ref.shape[1]
    shard = shard_refs[0].shape[1]
    rope = full - latent
    prompt = shard * n_seq
    tok = keys_a.shape[0] - shard
    my_resp = lax.axis_index("resp")
    my_seq = lax.axis_index("seq")
    odd = (my_resp % 2) == 1

    middle = slice(shard, shard + keys_b.shape[0])
    late = slice(middle.stop, prompt)
    scale = scale_ref[...]
    for d, ref in enumerate(shard_refs):
        put_keys(keys_c, d * shard, latent, scaled_rows(ref[...], scale))
    keys_ref[:shard] = keys_a[:shard]
    keys_ref[middle] = keys_b[...]
    keys_ref[late] = keys_c[...]
    keys_ref[prompt:] = keys_a[shard:]

    for i in range(rows // STEP):
        at = pl.ds(i * STEP, STEP)
        logits, dprob = partial_softmax(keys_c, at, q_ref, qr_ref, up_ref)
        before = stat_ref[0:1, at]
        top = jnp.maximum(before, jnp.max(logits, axis=0, keepdims=True))
        expo = jnp.exp2((logits - top) * EXP_SCALE)
        again = jnp.exp2((before - top) * EXP_SCALE)
        total = stat_ref[1:2, at] * again + jnp.sum(expo, axis=0, keepdims=True)
        weighed = stat_ref[2:3, at] * again + jnp.sum(expo * dprob, axis=0, keepdims=True)
        inverse = 1.0 / total
        delta = weighed * inverse
        factor = inverse * stat_ref[3:4, at]
        probs = expo * factor
        p_scr[late, at] = probs.astype(BF16)
        ds_ref[late, at] = (probs * (dprob - delta)).astype(BF16)
        probs = expo_b[:, at] * (factor * again)
        p_scr[middle, at] = probs.astype(BF16)
        ds_ref[middle, at] = (probs * (dprob_b[:, at] - delta)).astype(BF16)
        first = jnp.exp2((stat_ref[4:5, at] - top) * EXP_SCALE)
        probs = expo_a[:, at] * (factor * first)
        dscore = probs * (dprob_a[:, at] - delta)
        p_scr[:shard, at] = probs[:shard].astype(BF16)
        ds_ref[:shard, at] = dscore[:shard].astype(BF16)
        p_scr[prompt:, at] = probs[shard:].astype(BF16)
        ds_ref[prompt:, at] = dscore[shard:].astype(BF16)

    grad_latent = dot(ds_ref[...], q_ref[...], NN) + dot(p_scr[...], up_ref[...], NN)
    grad_rope = dot(ds_ref[...], qr_ref[...], NN)

    piece = tok // n_seq
    own_rope = grad_rope[prompt:]
    own_rope = own_rope + pltpu.roll(own_rope, rope, 1)
    for s in range(n_seq):
        parts = [
            grad_latent[prompt + s * piece : prompt + (s + 1) * piece, c : c + 2 * rope]
            for c in range(0, latent, 2 * rope)
        ]
        parts.append(own_rope[s * piece : (s + 1) * piece])
        span_out[s ^ my_seq] = jnp.concatenate(parts, axis=0).astype(BF16)

    cols = full // n_resp
    my_pair = my_resp // 2
    scale_twice = jnp.concatenate([scale[:, latent:]] * 2, axis=1)
    pairs = n_seq // 2 - 1
    for slot in range(n_seq):
        at = slice(slot * shard, (slot + 1) * shard)
        lat = (grad_latent[at] * scale[:, :latent]).T
        rot = (grad_rope[at] * scale_twice).T
        whole = jnp.concatenate([lat, rot[:rope] + rot[rope:]], axis=0)
        for z in range(n_resp // 2):
            even_part = whole[2 * z * cols : (2 * z + 1) * cols]
            odd_part = whole[(2 * z + 1) * cols : (2 * z + 2) * cols]
            mine = jnp.where(odd, odd_part, even_part).astype(BF16)
            theirs = jnp.where(odd, even_part, odd_part).astype(BF16)
            if slot in (0, n_seq - 1):
                d = slot
            elif slot <= pairs:
                d = 2 * slot - 1 + my_resp % 2
            else:
                d = 2 * (slot - pairs) - my_resp % 2
            mine_ref[d, z ^ my_pair] = mine
            if slot == n_seq - 1:
                far_ref[z ^ my_pair] = theirs
            else:
                theirs_ref[d, z ^ my_pair] = theirs


def sum_kernel(mine_ref, theirs_ref, span_ref, own_ref, *pay_refs):
    pairs = mine_ref.shape[1]
    for d in range(len(pay_refs) + 1):
        totals = [
            mine_ref[d, z].astype(F32) + theirs_ref[d, z].astype(F32) for z in range(pairs)
        ]
        if d == 0:
            for z in range(pairs):
                own_ref[z] = totals[z]
        else:
            totals.append(span_ref[d].astype(F32))
            pay_refs[d - 1][...] = jnp.concatenate(totals, axis=0).astype(BF16)


def query_kernel(
    heads, ds_ref, keys_ref, out_hbm, rope_hbm, out_v, rope_v, rope_scr, out_sems, rope_sems
):
    latent = out_v.shape[1]
    rope = (keys_ref.shape[1] - latent) // 2
    step = 16 * heads
    low = low_half((16, 2 * rope), rope)
    copies = []
    for i in range(out_v.shape[0] // step):
        at = pl.ds(i * step, step)
        out_v[at, :] = dot(ds_ref[:, at], keys_ref[:, :latent], TN).astype(BF16)
        copies.append(pltpu.make_async_copy(out_v.at[at], out_hbm.at[at], out_sems.at[i]))
        copies[-1].start()
        rope_scr[...] = dot(ds_ref[:, at], keys_ref[:, latent:], TN)
        for j in range(heads // 2):
            even = rope_scr[pl.ds(2 * j, 16, stride=heads), :]
            odd = rope_scr[pl.ds(2 * j + 1, 16, stride=heads), :]
            rope_v[pl.ds(i * 16, 16), pl.ds(2 * rope * j, 2 * rope)] = jnp.where(
                low, even, odd
            ).astype(BF16)
        copies.append(
            pltpu.make_async_copy(
                rope_v.at[pl.ds(i * 16, 16)],
                rope_hbm.at[pl.ds(i * 16, 16)],
                rope_sems.at[i],
            )
        )
        copies[-1].start()
    for copy in copies:
        copy.wait()


def on_device(
    n_resp,
    n_seq,
    prompt_cache,
    channel_scale,
    span_cache,
    q_latent,
    q_rope,
    d_out,
    resp_length,
    span_response,
    span_index,
):
    tok, heads, latent = q_latent.shape
    shard, full = prompt_cache.shape
    rope = full - latent
    rows = tok * heads
    prompt = shard * n_seq
    keys = prompt + tok
    early = shard + tok
    width = latent + 2 * rope
    cols = full // n_resp
    pairs = n_resp // 2
    piece = tok // n_seq
    span_rows = piece * (latent // (2 * rope) + 1)
    vmem = pl.BlockSpec(memory_space=pltpu.VMEM)
    hbm = pl.BlockSpec(memory_space=pl.ANY)

    def shape(dims, dtype=BF16):
        return jax.ShapeDtypeStruct(dims, dtype)

    def over_seq(x, d):
        return lax.ppermute(x, "seq", [(i, i ^ d) for i in range(n_seq)])

    def over_resp(x, d):
        return lax.ppermute(x, "resp", [(i, i ^ d) for i in range(n_resp)])

    def by_core(x, d):
        moves = [
            (r * n_seq + s, r * n_seq + (s ^ (d + r % 2)))
            for r in range(n_resp)
            for s in range(n_seq)
        ]
        return lax.ppermute(x, ("resp", "seq"), moves)

    prompt_t = prompt_cache.T
    fetched = [by_core(prompt_t, d) for d in range(1, n_seq - 1, 2)]

    scale_row = channel_scale.reshape(1, full)
    smem = pl.BlockSpec(memory_space=pltpu.SMEM)
    q_rows = q_latent.reshape(rows, latent)
    up_rows = d_out.reshape(rows, latent)
    mask = pl.pallas_call(
        functools.partial(mask_kernel, heads),
        out_shape=shape((tok, rows), F32),
        out_specs=vmem,
        compiler_params=pltpu.CompilerParams(vmem_limit_bytes=4 * MIB),
        cost_estimate=pl.CostEstimate(
            flops=40 * keys * rows * width, bytes_accessed=4 * tok * rows, transcendentals=0
        ),
        name="mask",
    )()
    again, mask = lax.optimization_barrier((prompt_t, mask))
    last = over_seq(again, n_seq - 1)
    q_turned, expo, dprob, stats, early_keys = pl.pallas_call(
        functools.partial(early_kernel, heads),
        out_shape=(
            shape((rows, 2 * rope)),
            shape((early, rows), F32),
            shape((early, rows), F32),
            shape((8, rows), F32),
            shape((early, width)),
        ),
        in_specs=[smem] * 3 + [vmem] * 7,
        out_specs=(vmem,) * 5,
        scratch_shapes=[pltpu.VMEM((rows, 2 * rope), F32)],
        compiler_params=pltpu.CompilerParams(vmem_limit_bytes=24 * MIB),
        cost_estimate=pl.CostEstimate(
            flops=2 * early * rows * 2 * latent, bytes_accessed=4 * rows * latent, transcendentals=0
        ),
        name="early",
    )(
        resp_length,
        span_response,
        span_index,
        mask,
        scale_row,
        prompt_t,
        span_cache,
        q_rows,
        q_rope,
        up_rows,
    )

    fetched, stats = lax.optimization_barrier((fetched, stats))
    swapped = [over_resp(value, 1) for value in fetched]
    middle = shard * len(fetched)
    expo_b, dprob_b, stats, middle_keys = pl.pallas_call(
        middle_kernel,
        out_shape=(
            shape((middle, rows), F32),
            shape((middle, rows), F32),
            shape((8, rows), F32),
            shape((middle, width)),
        ),
        in_specs=[vmem] * (5 + len(fetched)),
        out_specs=(vmem,) * 4,
        compiler_params=pltpu.CompilerParams(vmem_limit_bytes=24 * MIB),
        cost_estimate=pl.CostEstimate(
            flops=2 * middle * rows * 2 * latent, bytes_accessed=4 * rows * latent, transcendentals=0
        ),
        name="middle",
    )(scale_row, q_rows, up_rows, q_turned, stats, *fetched)

    mine, theirs, far, span, dscore, keys_all = pl.pallas_call(
        functools.partial(keys_kernel, n_resp, n_seq),
        out_shape=(
            shape((n_seq, pairs, cols, shard)),
            shape((n_seq - 1, pairs, cols, shard)),
            shape((pairs, cols, shard)),
            shape((n_seq, span_rows, 2 * rope)),
            shape((keys, rows)),
            shape((keys, width)),
        ),
        in_specs=[vmem] * (12 + len(swapped)),
        out_specs=(vmem,) * 6,
        scratch_shapes=[
            pltpu.VMEM((keys, rows), BF16),
            pltpu.VMEM((shard * (len(swapped) + 1), width), BF16),
        ],
        compiler_params=pltpu.CompilerParams(vmem_limit_bytes=24 * MIB),
        cost_estimate=pl.CostEstimate(
            flops=2 * keys * rows * 3 * latent, bytes_accessed=4 * rows * latent, transcendentals=0
        ),
        name="keys",
    )(
        scale_row,
        q_rows,
        up_rows,
        q_turned,
        expo,
        dprob,
        early_keys,
        expo_b,
        dprob_b,
        middle_keys,
        stats,
        *swapped,
        last,
    )

    steps = tok // 16

    def queries(dscore, keys_all):
        return pl.pallas_call(
            functools.partial(query_kernel, heads),
            out_shape=(shape((rows, latent)), shape((tok, heads * rope))),
            in_specs=[vmem] * 2,
            out_specs=(hbm,) * 2,
            scratch_shapes=[
                pltpu.VMEM((rows, latent), BF16),
                pltpu.VMEM((tok, heads * rope), BF16),
                pltpu.VMEM((16 * heads, 2 * rope), F32),
                pltpu.SemaphoreType.DMA((steps,)),
                pltpu.SemaphoreType.DMA((steps,)),
            ],
            compiler_params=pltpu.CompilerParams(vmem_limit_bytes=16 * MIB),
            cost_estimate=pl.CostEstimate(
                flops=2 * keys * rows * width, bytes_accessed=2 * rows * width, transcendentals=0
            ),
            name="queries",
        )(dscore, keys_all)

    far = over_resp(far, 1)
    theirs = over_resp(theirs, 1)
    farthest = mine[-1].astype(F32) + far.astype(F32)
    farthest = jnp.concatenate(
        [farthest.astype(BF16).reshape(-1, 2 * rope), span[-1]], axis=0
    )
    moved = [over_seq(farthest, n_seq - 1)]
    block, *pays = pl.pallas_call(
        sum_kernel,
        out_shape=[shape((pairs, cols, shard), F32)]
        + [shape((pairs * cols + span_rows, shard))] * (n_seq - 2),
        in_specs=[vmem] * 3,
        out_specs=[vmem] * (n_seq - 1),
        compiler_params=pltpu.CompilerParams(vmem_limit_bytes=8 * MIB),
        cost_estimate=pl.CostEstimate(
            flops=keys * rows * width, bytes_accessed=4 * keys * width, transcendentals=0
        ),
        name="sums",
    )(mine, theirs, span)
    moved += [over_seq(pay, d + 1) for d, pay in enumerate(pays)]
    grad_latent, grad_rope = queries(dscore, keys_all)
    split = pairs * cols
    own = span[0].astype(F32)
    for x in moved:
        block = block + x[:split].reshape(pairs, cols, shard).astype(F32)
        own = own + x[split:].astype(F32)
    block_half = block.astype(BF16)
    arrived = [over_resp(block_half[d], 2 * d) for d in range(pairs - 1, 0, -1)]
    total = block[0]
    for x in arrived:
        total = total + x.astype(F32)
    grad_prompt = total.T

    parts = own.reshape(-1, piece, 2 * rope)
    grad_span = jnp.concatenate(
        [parts[i] for i in range(latent // (2 * rope))] + [parts[-1][:, :rope]], axis=1
    )
    return (
        grad_latent.reshape(tok, heads, latent),
        grad_rope,
        grad_prompt,
        grad_span,
    )


def solution(mesh):
    return jax.shard_map(
        functools.partial(on_device, mesh.shape["resp"], mesh.shape["seq"]),
        mesh=mesh,
        in_specs=(
            P("seq", None),
            P(),
            P("resp", None),
            P("resp", "seq", None),
            P("resp", "seq"),
            P("resp", "seq", None),
            P(),
            P(),
            P(),
        ),
        out_specs=(
            P("resp", "seq", None),
            P("resp", "seq"),
            P("seq", "resp"),
            P(("resp", "seq"), None),
        ),
        check_vma=False,
    )
```

```python
import functools
import math

import jax
import jax.numpy as jnp
from jax import lax
from jax.experimental import pallas as pl
from jax.experimental.pallas import tpu as pltpu
from jax.sharding import PartitionSpec as P

SIGMA = 1.0 / math.sqrt(192.0)
EXP_SCALE = SIGMA * math.log2(math.e)
F32 = jnp.float32
BF16 = jnp.bfloat16
NT = (((1,), (1,)), ((), ()))
NN = (((1,), (0,)), ((), ()))
TN = (((0,), (0,)), ((), ()))
MIB = 1024 * 1024
STEP = 256


def dot(a, b, dims):
    return lax.dot_general(a, b, dims, preferred_element_type=F32)


def low_half(shape, half):
    return lax.broadcasted_iota(jnp.int32, shape, len(shape) - 1) < half


def put_keys(keys_ref, start, latent, values):
    rows, full = values.shape
    keys_ref[pl.ds(start, rows), :full] = values
    keys_ref[pl.ds(start, rows), full:] = values[:, latent:]


def scaled_rows(shard, scale):
    return (shard.astype(F32).T * scale).astype(BF16)


def mask_kernel(heads, mask_ref):
    key_pos = lax.broadcasted_iota(jnp.int32, mask_ref.shape, 0)
    row = lax.broadcasted_iota(jnp.int32, mask_ref.shape, 1)
    mask_ref[...] = jnp.where(key_pos * heads <= row, 1.0, 0.0)


def partial_softmax(keys_ref, at, q_ref, qr_ref, up_ref):
    latent = q_ref.shape[1]
    logits = dot(keys_ref[:, :latent], q_ref[at, :], NT) + dot(
        keys_ref[:, latent:], qr_ref[at, :], NT
    )
    return logits, dot(keys_ref[:, :latent], up_ref[at, :], NT) * SIGMA


def early_kernel(
    heads,
    length_s,
    response_s,
    index_s,
    mask_ref,
    scale_ref,
    prompt_ref,
    span_ref,
    q_ref,
    qrope_v,
    up_ref,
    qr_ref,
    expo_ref,
    dprob_ref,
    stat_ref,
    keys_ref,
    rope_scr,
):
    full, shard = prompt_ref.shape
    tok = span_ref.shape[0]
    rows, latent = q_ref.shape
    rope = full - latent
    my_resp = lax.axis_index("resp")
    live = jnp.clip(
        length_s[response_s[my_resp]] - index_s[my_resp] * tok, 0, tok
    )
    low = low_half((tok, 2 * rope), rope)
    for j in range(heads // 2):
        x = qrope_v[:, pl.ds(2 * rope * j, 2 * rope)].astype(F32)
        rope_scr[pl.ds(2 * j, tok, stride=heads), :] = jnp.where(low, x, 0.0)
        rope_scr[pl.ds(2 * j + 1, tok, stride=heads), :] = jnp.where(low, 0.0, x)
    qr_ref[...] = rope_scr[...].astype(BF16)

    put_keys(keys_ref, 0, latent, scaled_rows(prompt_ref[...], scale_ref[...]))
    put_keys(keys_ref, shard, latent, span_ref[...])

    for i in range(rows // STEP):
        at = pl.ds(i * STEP, STEP)
        logits, dprob = partial_softmax(keys_ref, at, q_ref, qr_ref, up_ref)
        key_pos = lax.broadcasted_iota(jnp.int32, (tok, STEP), 0)
        seen = (mask_ref[:, at] > 0.5) & (key_pos < live)
        own = jnp.where(seen, logits[shard:], -jnp.inf)
        logits = jnp.concatenate([logits[:shard], own], axis=0)
        top = jnp.max(logits, axis=0, keepdims=True)
        expo = jnp.exp2((logits - top) * EXP_SCALE)
        row_pos = (lax.broadcasted_iota(jnp.int32, (1, STEP), 1) + i * STEP) // heads
        expo_ref[:, at] = expo
        dprob_ref[:, at] = dprob
        stat_ref[0:1, at] = top
        stat_ref[1:2, at] = jnp.sum(expo, axis=0, keepdims=True)
        stat_ref[2:3, at] = jnp.sum(expo * dprob, axis=0, keepdims=True)
        stat_ref[3:4, at] = jnp.where(row_pos < live, 1.0, 0.0)


def middle_kernel(scale_ref, q_ref, up_ref, qr_ref, stat_ref, *refs):
    shard_refs = refs[:-4]
    expo_ref, dprob_ref, out_ref, keys_ref = refs[-4:]
    rows, latent = q_ref.shape
    shard = shard_refs[0].shape[1]
    for d, ref in enumerate(shard_refs):
        put_keys(keys_ref, d * shard, latent, scaled_rows(ref[...], scale_ref[...]))
    for i in range(rows // STEP):
        at = pl.ds(i * STEP, STEP)
        logits, dprob = partial_softmax(keys_ref, at, q_ref, qr_ref, up_ref)
        before = stat_ref[0:1, at]
        top = jnp.maximum(before, jnp.max(logits, axis=0, keepdims=True))
        expo = jnp.exp2((logits - top) * EXP_SCALE)
        again = jnp.exp2((before - top) * EXP_SCALE)
        expo_ref[:, at] = expo
        dprob_ref[:, at] = dprob
        out_ref[0:1, at] = top
        out_ref[1:2, at] = stat_ref[1:2, at] * again + jnp.sum(expo, axis=0, keepdims=True)
        out_ref[2:3, at] = stat_ref[2:3, at] * again + jnp.sum(
            expo * dprob, axis=0, keepdims=True
        )
        out_ref[3:4, at] = stat_ref[3:4, at]
        out_ref[4:5, at] = before


def keys_kernel(
    n_resp,
    n_seq,
    scale_ref,
    q_ref,
    up_ref,
    qr_ref,
    expo_a,
    dprob_a,
    keys_a,
    expo_b,
    dprob_b,
    keys_b,
    stat_ref,
    *refs,
):
    shard_refs = refs[:-8]
    mine_ref, theirs_ref, far_ref, span_out, ds_ref, keys_ref, p_scr, keys_c = refs[-8:]
    rows, latent = q_ref.shape
    full = scale_ref.shape[1]
    shard = shard_refs[0].shape[1]
    rope = full - latent
    prompt = shard * n_seq
    tok = keys_a.shape[0] - shard
    my_resp = lax.axis_index("resp")
    my_seq = lax.axis_index("seq")
    odd = (my_resp % 2) == 1

    middle = slice(shard, shard + keys_b.shape[0])
    late = slice(middle.stop, prompt)
    scale = scale_ref[...]
    for d, ref in enumerate(shard_refs):
        put_keys(keys_c, d * shard, latent, scaled_rows(ref[...], scale))
    keys_ref[:shard] = keys_a[:shard]
    keys_ref[middle] = keys_b[...]
    keys_ref[late] = keys_c[...]
    keys_ref[prompt:] = keys_a[shard:]

    for i in range(rows // STEP):
        at = pl.ds(i * STEP, STEP)
        logits, dprob = partial_softmax(keys_c, at, q_ref, qr_ref, up_ref)
        before = stat_ref[0:1, at]
        top = jnp.maximum(before, jnp.max(logits, axis=0, keepdims=True))
        expo = jnp.exp2((logits - top) * EXP_SCALE)
        again = jnp.exp2((before - top) * EXP_SCALE)
        total = stat_ref[1:2, at] * again + jnp.sum(expo, axis=0, keepdims=True)
        weighed = stat_ref[2:3, at] * again + jnp.sum(expo * dprob, axis=0, keepdims=True)
        inverse = 1.0 / total
        delta = weighed * inverse
        factor = inverse * stat_ref[3:4, at]
        probs = expo * factor
        p_scr[late, at] = probs.astype(BF16)
        ds_ref[late, at] = (probs * (dprob - delta)).astype(BF16)
        probs = expo_b[:, at] * (factor * again)
        p_scr[middle, at] = probs.astype(BF16)
        ds_ref[middle, at] = (probs * (dprob_b[:, at] - delta)).astype(BF16)
        first = jnp.exp2((stat_ref[4:5, at] - top) * EXP_SCALE)
        probs = expo_a[:, at] * (factor * first)
        dscore = probs * (dprob_a[:, at] - delta)
        p_scr[:shard, at] = probs[:shard].astype(BF16)
        ds_ref[:shard, at] = dscore[:shard].astype(BF16)
        p_scr[prompt:, at] = probs[shard:].astype(BF16)
        ds_ref[prompt:, at] = dscore[shard:].astype(BF16)

    grad_latent = dot(ds_ref[...], q_ref[...], NN) + dot(p_scr[...], up_ref[...], NN)
    grad_rope = dot(ds_ref[...], qr_ref[...], NN)

    piece = tok // n_seq
    own_rope = grad_rope[prompt:]
    own_rope = own_rope + pltpu.roll(own_rope, rope, 1)
    for s in range(n_seq):
        parts = [
            grad_latent[prompt + s * piece : prompt + (s + 1) * piece, c : c + 2 * rope]
            for c in range(0, latent, 2 * rope)
        ]
        parts.append(own_rope[s * piece : (s + 1) * piece])
        span_out[s ^ my_seq] = jnp.concatenate(parts, axis=0).astype(BF16)

    cols = full // n_resp
    my_pair = my_resp // 2
    scale_twice = jnp.concatenate([scale[:, latent:]] * 2, axis=1)
    pairs = n_seq // 2 - 1
    for slot in range(n_seq):
        at = slice(slot * shard, (slot + 1) * shard)
        lat = (grad_latent[at] * scale[:, :latent]).T
        rot = (grad_rope[at] * scale_twice).T
        whole = jnp.concatenate([lat, rot[:rope] + rot[rope:]], axis=0)
        for z in range(n_resp // 2):
            even_part = whole[2 * z * cols : (2 * z + 1) * cols]
            odd_part = whole[(2 * z + 1) * cols : (2 * z + 2) * cols]
            mine = jnp.where(odd, odd_part, even_part).astype(BF16)
            theirs = jnp.where(odd, even_part, odd_part).astype(BF16)
            if slot in (0, n_seq - 1):
                d = slot
            elif slot <= pairs:
                d = 2 * slot - 1 + my_resp % 2
            else:
                d = 2 * (slot - pairs) - my_resp % 2
            mine_ref[d, z ^ my_pair] = mine
            if slot == n_seq - 1:
                far_ref[z ^ my_pair] = theirs
            else:
                theirs_ref[d, z ^ my_pair] = theirs


def sum_kernel(mine_ref, theirs_ref, span_ref, own_ref, *pay_refs):
    pairs = mine_ref.shape[1]
    for d in range(len(pay_refs) + 1):
        totals = [
            mine_ref[d, z].astype(F32) + theirs_ref[d, z].astype(F32) for z in range(pairs)
        ]
        if d == 0:
            for z in range(pairs):
                own_ref[z] = totals[z]
        else:
            totals.append(span_ref[d].astype(F32))
            pay_refs[d - 1][...] = jnp.concatenate(totals, axis=0).astype(BF16)


def query_kernel(
    heads, ds_ref, keys_ref, out_hbm, rope_hbm, out_v, rope_v, rope_scr, out_sems, rope_sems
):
    latent = out_v.shape[1]
    rope = (keys_ref.shape[1] - latent) // 2
    step = 16 * heads
    low = low_half((16, 2 * rope), rope)
    copies = []
    for i in range(out_v.shape[0] // step):
        at = pl.ds(i * step, step)
        out_v[at, :] = dot(ds_ref[:, at], keys_ref[:, :latent], TN).astype(BF16)
        copies.append(pltpu.make_async_copy(out_v.at[at], out_hbm.at[at], out_sems.at[i]))
        copies[-1].start()
        rope_scr[...] = dot(ds_ref[:, at], keys_ref[:, latent:], TN)
        for j in range(heads // 2):
            even = rope_scr[pl.ds(2 * j, 16, stride=heads), :]
            odd = rope_scr[pl.ds(2 * j + 1, 16, stride=heads), :]
            rope_v[pl.ds(i * 16, 16), pl.ds(2 * rope * j, 2 * rope)] = jnp.where(
                low, even, odd
            ).astype(BF16)
        copies.append(
            pltpu.make_async_copy(
                rope_v.at[pl.ds(i * 16, 16)],
                rope_hbm.at[pl.ds(i * 16, 16)],
                rope_sems.at[i],
            )
        )
        copies[-1].start()
    for copy in copies:
        copy.wait()


def on_device(
    n_resp,
    n_seq,
    prompt_cache,
    channel_scale,
    span_cache,
    q_latent,
    q_rope,
    d_out,
    resp_length,
    span_response,
    span_index,
):
    tok, heads, latent = q_latent.shape
    shard, full = prompt_cache.shape
    rope = full - latent
    rows = tok * heads
    prompt = shard * n_seq
    keys = prompt + tok
    early = shard + tok
    width = latent + 2 * rope
    cols = full // n_resp
    pairs = n_resp // 2
    piece = tok // n_seq
    span_rows = piece * (latent // (2 * rope) + 1)
    vmem = pl.BlockSpec(memory_space=pltpu.VMEM)
    hbm = pl.BlockSpec(memory_space=pl.ANY)

    def shape(dims, dtype=BF16):
        return jax.ShapeDtypeStruct(dims, dtype)

    def over_seq(x, d):
        return lax.ppermute(x, "seq", [(i, i ^ d) for i in range(n_seq)])

    def over_resp(x, d):
        return lax.ppermute(x, "resp", [(i, i ^ d) for i in range(n_resp)])

    def by_core(x, d):
        moves = [
            (r * n_seq + s, r * n_seq + (s ^ (d + r % 2)))
            for r in range(n_resp)
            for s in range(n_seq)
        ]
        return lax.ppermute(x, ("resp", "seq"), moves)

    prompt_t = prompt_cache.T
    fetched = [by_core(prompt_t, d) for d in range(1, n_seq - 1, 2)]

    scale_row = channel_scale.reshape(1, full)
    smem = pl.BlockSpec(memory_space=pltpu.SMEM)
    q_rows = q_latent.reshape(rows, latent)
    up_rows = d_out.reshape(rows, latent)
    mask = pl.pallas_call(
        functools.partial(mask_kernel, heads),
        out_shape=shape((tok, rows), F32),
        out_specs=vmem,
        compiler_params=pltpu.CompilerParams(vmem_limit_bytes=4 * MIB),
        cost_estimate=pl.CostEstimate(
            flops=40 * keys * rows * width, bytes_accessed=4 * tok * rows, transcendentals=0
        ),
        name="mask",
    )()
    again, mask = lax.optimization_barrier((prompt_t, mask))
    last = over_seq(again, n_seq - 1)
    q_turned, expo, dprob, stats, early_keys = pl.pallas_call(
        functools.partial(early_kernel, heads),
        out_shape=(
            shape((rows, 2 * rope)),
            shape((early, rows), F32),
            shape((early, rows), F32),
            shape((8, rows), F32),
            shape((early, width)),
        ),
        in_specs=[smem] * 3 + [vmem] * 7,
        out_specs=(vmem,) * 5,
        scratch_shapes=[pltpu.VMEM((rows, 2 * rope), F32)],
        compiler_params=pltpu.CompilerParams(vmem_limit_bytes=24 * MIB),
        cost_estimate=pl.CostEstimate(
            flops=2 * early * rows * 2 * latent, bytes_accessed=4 * rows * latent, transcendentals=0
        ),
        name="early",
    )(
        resp_length,
        span_response,
        span_index,
        mask,
        scale_row,
        prompt_t,
        span_cache,
        q_rows,
        q_rope,
        up_rows,
    )

    fetched, stats = lax.optimization_barrier((fetched, stats))
    swapped = [over_resp(value, 1) for value in fetched]
    middle = shard * len(fetched)
    expo_b, dprob_b, stats, middle_keys = pl.pallas_call(
        middle_kernel,
        out_shape=(
            shape((middle, rows), F32),
            shape((middle, rows), F32),
            shape((8, rows), F32),
            shape((middle, width)),
        ),
        in_specs=[vmem] * (5 + len(fetched)),
        out_specs=(vmem,) * 4,
        compiler_params=pltpu.CompilerParams(vmem_limit_bytes=24 * MIB),
        cost_estimate=pl.CostEstimate(
            flops=2 * middle * rows * 2 * latent, bytes_accessed=4 * rows * latent, transcendentals=0
        ),
        name="middle",
    )(scale_row, q_rows, up_rows, q_turned, stats, *fetched)

    mine, theirs, far, span, dscore, keys_all = pl.pallas_call(
        functools.partial(keys_kernel, n_resp, n_seq),
        out_shape=(
            shape((n_seq, pairs, cols, shard)),
            shape((n_seq - 1, pairs, cols, shard)),
            shape((pairs, cols, shard)),
            shape((n_seq, span_rows, 2 * rope)),
            shape((keys, rows)),
            shape((keys, width)),
        ),
        in_specs=[vmem] * (12 + len(swapped)),
        out_specs=(vmem,) * 6,
        scratch_shapes=[
            pltpu.VMEM((keys, rows), BF16),
            pltpu.VMEM((shard * (len(swapped) + 1), width), BF16),
        ],
        compiler_params=pltpu.CompilerParams(vmem_limit_bytes=24 * MIB),
        cost_estimate=pl.CostEstimate(
            flops=2 * keys * rows * 3 * latent, bytes_accessed=4 * rows * latent, transcendentals=0
        ),
        name="keys",
    )(
        scale_row,
        q_rows,
        up_rows,
        q_turned,
        expo,
        dprob,
        early_keys,
        expo_b,
        dprob_b,
        middle_keys,
        stats,
        *swapped,
        last,
    )

    steps = tok // 16

    def queries(dscore, keys_all):
        return pl.pallas_call(
            functools.partial(query_kernel, heads),
            out_shape=(shape((rows, latent)), shape((tok, heads * rope))),
            in_specs=[vmem] * 2,
            out_specs=(hbm,) * 2,
            scratch_shapes=[
                pltpu.VMEM((rows, latent), BF16),
                pltpu.VMEM((tok, heads * rope), BF16),
                pltpu.VMEM((16 * heads, 2 * rope), F32),
                pltpu.SemaphoreType.DMA((steps,)),
                pltpu.SemaphoreType.DMA((steps,)),
            ],
            compiler_params=pltpu.CompilerParams(vmem_limit_bytes=16 * MIB),
            cost_estimate=pl.CostEstimate(
                flops=2 * keys * rows * width, bytes_accessed=2 * rows * width, transcendentals=0
            ),
            name="queries",
        )(dscore, keys_all)

    far = over_resp(far, 1)
    theirs = over_resp(theirs, 1)
    farthest = mine[-1].astype(F32) + far.astype(F32)
    farthest = jnp.concatenate(
        [farthest.astype(BF16).reshape(-1, 2 * rope), span[-1]], axis=0
    )
    moved = [over_seq(farthest, n_seq - 1)]
    block, *pays = pl.pallas_call(
        sum_kernel,
        out_shape=[shape((pairs, cols, shard), F32)]
        + [shape((pairs * cols + span_rows, shard))] * (n_seq - 2),
        in_specs=[vmem] * 3,
        out_specs=[vmem] * (n_seq - 1),
        compiler_params=pltpu.CompilerParams(vmem_limit_bytes=8 * MIB),
        cost_estimate=pl.CostEstimate(
            flops=keys * rows * width, bytes_accessed=4 * keys * width, transcendentals=0
        ),
        name="sums",
    )(mine, theirs, span)
    moved += [over_seq(pay, d + 1) for d, pay in enumerate(pays)]
    grad_latent, grad_rope = queries(dscore, keys_all)
    split = pairs * cols
    own = span[0].astype(F32)
    for x in moved:
        block = block + x[:split].reshape(pairs, cols, shard).astype(F32)
        own = own + x[split:].astype(F32)
    block_half = block.astype(BF16)
    order = sorted(range(1, pairs), key=lambda d: (d != pairs // 2, d))
    arrived = [over_resp(block_half[d], 2 * d) for d in order]
    total = block[0]
    for x in arrived:
        total = total + x.astype(F32)
    grad_prompt = total.T

    parts = own.reshape(-1, piece, 2 * rope)
    grad_span = jnp.concatenate(
        [parts[i] for i in range(latent // (2 * rope))] + [parts[-1][:, :rope]], axis=1
    )
    return (
        grad_latent.reshape(tok, heads, latent),
        grad_rope,
        grad_prompt,
        grad_span,
    )


def solution(mesh):
    return jax.shard_map(
        functools.partial(on_device, mesh.shape["resp"], mesh.shape["seq"]),
        mesh=mesh,
        in_specs=(
            P("seq", None),
            P(),
            P("resp", None),
            P("resp", "seq", None),
            P("resp", "seq"),
            P("resp", "seq", None),
            P(),
            P(),
            P(),
        ),
        out_specs=(
            P("resp", "seq", None),
            P("resp", "seq"),
            P("seq", "resp"),
            P(("resp", "seq"), None),
        ),
        check_vma=False,
    )
```
